256 devices in a mesh: sec: 32 (over z, x_lo, core), tp: 8 (over x_hi, y).
Axes of the slice: x: 4 (x_hi: 2, x_lo: 2; x = x_hi * 2 + x_lo), y: 4, z: 8, core: 2. Of those that a mesh axis runs over, the one named last changes fastest.
Arguments:
- patches: bfloat16 [1024, 5120], P('sec', 'tp'), may hold values from -6 to 6
- merge_gain: float32 [1280], replicated, may hold values from 0.5 to 1.5
- merge_bias: float32 [1280], replicated, may hold values from -2 to 2
- merge_inner: bfloat16 [5120, 3072], P(None, 'tp'), may hold values from -0.078125 to 0.078125
- merge_outer: bfloat16 [3072, 8192], P('tp'), may hold values from -0.109375 to 0.109375
- slot_target: int32 [1024], replicated, may hold values from 0 to 4095, as said below
- text_embed: bfloat16 [2, 2048, 8192], P(None, 'sec', 'tp'), may hold values from -10 to 10
- norm_gain: float32 [8192], replicated, may hold values from 0.5 to 1.5
- query_weight: bfloat16 [8192, 4096], P('sec', 'tp'), may hold values from -0.03691997 to 0.03691997
- key_weight: bfloat16 [8192, 1024], P('sec', 'tp'), may hold values from -0.03691997 to 0.03691997
- value_weight: bfloat16 [8192, 1024], P('sec', 'tp'), may hold values from -0.0625 to 0.0625
- attn_cotangent: bfloat16 [2, 2048, 4096], P(None, 'sec', 'tp'), may hold values from -6 to 6
Outputs:
- attended: bfloat16 [2, 2048, 4096], P(None, 'sec', 'tp')
- grad_text: bfloat16 [2, 2048, 8192], P(None, 'sec', 'tp')
- grad_image: bfloat16 [1024, 8192], P('sec', 'tp')
The draws below stay inside these ranges and needn't reach their ends.
Inputs may be any that keep to these rules, and one draw needn't show every extreme that they name: `slot_target`: all values differ. Of the 64 positions of each micro-batch on each index of sec, exactly 16 are image places.
All inputs are finite; a program needn't handle non-finite values.
Results may differ from the reference program's by a relative error of at most 0.022.
Values may be sent and summed in bfloat16 or wider, within the bound.
A program may use at most 128 MiB of HBM per device.

```python
import math
import jax
import jax.numpy as jnp
from jax import lax

D = 8192
HEADS = 32
KV_HEADS = 8
HEAD_DIM = 128
VIT = 1280
MERGE_IN = 5120
MHID = 3072
MICRO = 2
TOK_MB = 64
IMG_MB = 16
SEQ = 2048
ROWS = 1024


def image_places(key):
    key = jax.random.fold_in(key, 11)
    owners = SEQ // TOK_MB
    blocks = owners * MICRO
    block_keys = jax.random.split(jax.random.fold_in(key, 1), blocks)
    chosen = jax.vmap(lambda block_key: jnp.sort(jax.random.permutation(block_key, TOK_MB)[:IMG_MB]))(block_keys)
    block_ids = jnp.arange(blocks, dtype=jnp.int32)
    base = block_ids % MICRO * SEQ + block_ids // MICRO * TOK_MB
    return (base[:, None] + chosen.astype(jnp.int32)).reshape(-1)


def projection_base(key, columns):
    return jnp.clip(jax.random.normal(key, (D, columns), jnp.float32), -3.0, 3.0) * D ** (-0.5)


def draw_slot_target(key, part):
    places = image_places(key)
    key = jax.random.fold_in(key, 12)
    order = jax.random.permutation(key, ROWS)
    return places[order].astype(jnp.int32)


def draw_query_weight(key, part):
    key = jax.random.fold_in(key, 31)
    weight = projection_base(key, HEADS * HEAD_DIM)
    return weight.astype(jnp.bfloat16)


def draw_key_weight(key, part):
    key = jax.random.fold_in(key, 32)
    weight = projection_base(key, KV_HEADS * HEAD_DIM)
    return weight.astype(jnp.bfloat16)


def draw_text_embed(key, part):
    key = jax.random.fold_in(key, 41)
    return jnp.clip(jax.random.normal(jax.random.fold_in(key, 1), (MICRO, SEQ, D), jnp.float32), -6.0, 6.0).astype(jnp.bfloat16)


def level_of(rng, dims, shards, smallest, high):
    gain = 1.0
    for dim, shards_of in shards:
        heights = jax.random.uniform(jax.random.fold_in(jax.random.fold_in(rng, 6), dim), (shards_of,), jnp.float32, smallest / len(shards), high / len(shards))
        gain = gain * jnp.repeat(jnp.exp(heights), dims[dim] // shards_of).reshape((-1,) + (1,) * (len(dims) - 1 - dim))
    return gain


def gaussian(rng, shape, scale, bound, cuts=(), held_as=jnp.bfloat16):
    values = scale * jax.random.normal(rng, shape, jnp.float32)
    if cuts:
        values = values * level_of(rng, shape, cuts, -0.22, 0.18)
    return jnp.clip(values, -bound, bound).astype(held_as)


def setup_inputs(seed: int = 0) -> dict:
    seeds = jax.random.split(jax.random.key(seed), 13)
    patches = gaussian(seeds[0], (ROWS, MERGE_IN), 1.0, 6.0, ((0, 32), (1, 8)))
    merge_gain = jnp.clip(1.0 + 0.1 * jax.random.normal(seeds[1], (VIT,), jnp.float32), 0.5, 1.5)
    merge_bias = gaussian(seeds[2], (VIT,), 0.3, 2.0, (), jnp.float32)
    merge_inner = gaussian(seeds[3], (MERGE_IN, MHID), MERGE_IN ** -0.5, 0.078125, ((1, 8),))
    merge_outer = gaussian(seeds[4], (MHID, D), MHID ** -0.5, 0.109375, ((0, 8),))
    slot_target = draw_slot_target(jax.random.fold_in(seeds[12], 71), 0)
    text_embed = draw_text_embed(jax.random.fold_in(seeds[12], 71), 0)
    norm_gain = jnp.clip(1.0 + 0.1 * jax.random.normal(seeds[7], (D,), jnp.float32), 0.5, 1.5)
    query_weight = draw_query_weight(jax.random.fold_in(seeds[12], 71), 0)
    key_weight = draw_key_weight(jax.random.fold_in(seeds[12], 71), 0)
    value_weight = gaussian(seeds[10], (D, KV_HEADS * HEAD_DIM), D ** -0.5, 0.0625, ((0, 32), (1, 8)))
    attn_cotangent = gaussian(seeds[11], (MICRO, SEQ, HEADS * HEAD_DIM), 1.0, 6.0, ((1, 32), (2, 8)))
    return dict(patches=patches, merge_gain=merge_gain, merge_bias=merge_bias, merge_inner=merge_inner, merge_outer=merge_outer, slot_target=slot_target, text_embed=text_embed, norm_gain=norm_gain, query_weight=query_weight, key_weight=key_weight, value_weight=value_weight, attn_cotangent=attn_cotangent)


def merge_rows(full_rows, merge_gain, merge_bias, merge_inner, merge_outer):
    row_count = full_rows.shape[0]
    pieces = full_rows.astype(jnp.float32).reshape(row_count, -1, merge_gain.shape[0])
    centre = lax.optimization_barrier(jnp.mean(pieces, axis=-1, keepdims=True))
    shifted = pieces - centre
    spread = lax.optimization_barrier(jnp.mean(shifted * shifted, axis=-1, keepdims=True))
    normed = (shifted * lax.rsqrt(spread + 1e-06) * merge_gain + merge_bias).reshape(row_count, -1).astype(jnp.bfloat16)
    hidden = jax.nn.gelu(jnp.dot(normed, merge_inner, preferred_element_type=jnp.float32), approximate=False).astype(jnp.bfloat16)
    return jnp.dot(hidden, merge_outer, preferred_element_type=jnp.float32)

def attend_group(operands, causal, score_scale):
    queries, keys_group, values_group, grad_out = operands
    queries_wide = queries.astype(jnp.float32)
    keys_wide = keys_group.astype(jnp.float32)
    values_wide = values_group.astype(jnp.float32)
    grad_wide = grad_out.astype(jnp.float32)
    scores = jnp.einsum('msgd,mtd->mgst', queries_wide, keys_wide) * score_scale
    scores = jnp.where(causal, scores, -1e+30)
    row_max = lax.optimization_barrier(jnp.max(scores, axis=-1, keepdims=True))
    raw_weights = jnp.exp(scores - row_max)
    attention_weights = raw_weights / lax.optimization_barrier(jnp.sum(raw_weights, axis=-1, keepdims=True))
    weights_half = attention_weights.astype(jnp.bfloat16)
    half_wide = weights_half.astype(jnp.float32)
    attended = jnp.einsum('mgst,mtd->msgd', half_wide, values_wide).astype(jnp.bfloat16)
    grad_weights = jnp.einsum('msgd,mtd->mgst', grad_wide, values_wide)
    row_delta = lax.optimization_barrier(jnp.sum(attention_weights * grad_weights, axis=-1, keepdims=True))
    grad_scores = (attention_weights * (grad_weights - row_delta)).astype(jnp.bfloat16).astype(jnp.float32)
    grad_q = (jnp.einsum('mgst,mtd->msgd', grad_scores, keys_wide) * score_scale).astype(jnp.bfloat16)
    grad_k = (jnp.einsum('mgst,msgd->mtd', grad_scores, queries_wide) * score_scale).astype(jnp.bfloat16)
    grad_v = jnp.einsum('mgst,msgd->mtd', half_wide, grad_wide).astype(jnp.bfloat16)
    return (attended, grad_q, grad_k, grad_v)

def reference(patches, merge_gain, merge_bias, merge_inner, merge_outer, slot_target, text_embed, norm_gain, query_weight, key_weight, value_weight, attn_cotangent):
    image_embed = merge_rows(patches, merge_gain, merge_bias, merge_inner, merge_outer).astype(jnp.bfloat16)
    places = MICRO * SEQ
    source = jnp.full((places,), -1, jnp.int32).at[slot_target].set(jnp.arange(ROWS, dtype=jnp.int32))
    is_image = source >= 0
    flat_text = text_embed.reshape(places, D)
    picked = jnp.take(image_embed, jnp.maximum(source, 0).astype(jnp.int32), axis=0)
    llm_input = jnp.where(is_image[:, None], picked, flat_text)
    input_wide = llm_input.astype(jnp.float32)
    inv_rms = lax.rsqrt(lax.optimization_barrier(jnp.mean(input_wide * input_wide, axis=-1, keepdims=True)) + 1e-06)
    normed = (input_wide * inv_rms * norm_gain).astype(jnp.bfloat16)
    group_size = HEADS // KV_HEADS
    queries = jnp.dot(normed, query_weight, preferred_element_type=jnp.float32).astype(jnp.bfloat16)
    queries = queries.reshape(MICRO, SEQ, KV_HEADS, group_size, HEAD_DIM).transpose(2, 0, 1, 3, 4)
    keys_all = jnp.dot(normed, key_weight, preferred_element_type=jnp.float32).astype(jnp.bfloat16)
    keys_all = keys_all.reshape(MICRO, SEQ, KV_HEADS, HEAD_DIM).transpose(2, 0, 1, 3)
    values_all = jnp.dot(normed, value_weight, preferred_element_type=jnp.float32).astype(jnp.bfloat16)
    values_all = values_all.reshape(MICRO, SEQ, KV_HEADS, HEAD_DIM).transpose(2, 0, 1, 3)
    grad_out = attn_cotangent.reshape(MICRO, SEQ, KV_HEADS, group_size, HEAD_DIM).transpose(2, 0, 1, 3, 4)
    seq_ids = jnp.arange(SEQ, dtype=jnp.int32)
    causal = seq_ids[None, :] <= seq_ids[:, None]
    score_scale = 1.0 / math.sqrt(HEAD_DIM)
    attended, grad_q, grad_k, grad_v = lax.map(lambda operands: attend_group(operands, causal, score_scale), (queries, keys_all, values_all, grad_out))
    attended = attended.transpose(1, 2, 0, 3, 4).reshape(MICRO, SEQ, HEADS * HEAD_DIM)
    grad_q = grad_q.transpose(1, 2, 0, 3, 4).reshape(places, HEADS * HEAD_DIM)
    grad_k = grad_k.transpose(1, 2, 0, 3).reshape(places, KV_HEADS * HEAD_DIM)
    grad_v = grad_v.transpose(1, 2, 0, 3).reshape(places, KV_HEADS * HEAD_DIM)
    grad_normed = jnp.dot(grad_q, query_weight.T, preferred_element_type=jnp.float32)
    grad_normed = grad_normed + jnp.dot(grad_k, key_weight.T, preferred_element_type=jnp.float32)
    grad_normed = grad_normed + jnp.dot(grad_v, value_weight.T, preferred_element_type=jnp.float32)
    scaled = grad_normed * norm_gain
    inner_sum = lax.optimization_barrier(jnp.sum(scaled * input_wide, axis=-1, keepdims=True))
    grad_input = (inv_rms * scaled - input_wide * inv_rms ** 3 * inner_sum / D).astype(jnp.bfloat16)
    grad_text = jnp.where(is_image[:, None], jnp.zeros_like(grad_input), grad_input).reshape(MICRO, SEQ, D)
    grad_image = jnp.take(grad_input, slot_target, axis=0)
    return (attended, grad_text, grad_image)
```

```python
import functools
import math

import jax
import jax.numpy as jnp
from jax import lax
from jax.experimental import pallas as pl
from jax.experimental.pallas import tpu as pltpu
from jax.sharding import PartitionSpec as P

HEAD_DIM = 128
BF = jnp.bfloat16
F32 = jnp.float32
MESH = pl.DeviceIdType.MESH


def dot_nn(a, b):
    return jnp.dot(a, b, preferred_element_type=F32)


def dot_nt(a, b):
    return lax.dot_general(a, b, (((1,), (1,)), ((), ())), preferred_element_type=F32)


def dot_tn(a, b):
    return lax.dot_general(a, b, (((0,), (0,)), ((), ())), preferred_element_type=F32)


def row_tile(column):
    return jnp.broadcast_to(column, (128, 128)).T[:8]


def column_of(tile):
    return jnp.broadcast_to(tile[0:1, :], (128, 128)).T


def kernel(nz, nt, ny, names, *refs):
    r = dict(zip(names, refs))
    patches, gain, bias, inner, outer = (r[n] for n in ("patches", "gain", "bias", "inner", "outer"))
    text, w, cot = r["text"], r["w"], r["cot"]
    ssem, rsem, lsem = r["ssem"], r["rsem"], r["lsem"]
    sec, t = lax.axis_index("sec"), lax.axis_index("tp")
    z, s4 = lax.div(sec, 4), lax.rem(sec, 4)
    xl, c = lax.div(s4, 2), lax.rem(s4, 2)
    nxh = nt // ny
    xh, y = lax.div(t, ny), lax.rem(t, ny)
    rows, pw = patches.shape
    chunk = text.shape[2] // 4
    plane = 4 * 128
    images = 4 * rows
    width = text.shape[2] * nt
    seq = nz * 256
    scale = 1.0 / math.sqrt(HEAD_DIM)

    def zmod(v):
        return lax.rem(v + nz, nz)

    def to_t(d):
        dx, dy = d // ny, d % ny
        return lax.rem(xh + dx, nxh) * ny + lax.rem(y + dy, ny)

    def from_t(d):
        dx, dy = d // ny, d % ny
        return lax.rem(xh + nxh - dx, nxh) * ny + lax.rem(y + ny - dy, ny)

    def near(k):
        a = 1 - xl if k // 2 else xl
        b = 1 - c if k % 2 else c
        return a, b

    def dev(zz, xx, cc, tt):
        return (zz * 4 + xx * 2 + cc, tt)

    counter = [0]
    pending = []

    def alloc(n):
        first = counter[0]
        counter[0] += n
        assert counter[0] <= r["n_sem"]
        return first

    def rcopy(src, dst, k, to):
        return pltpu.make_async_remote_copy(
            src_ref=src, dst_ref=dst, send_sem=ssem.at[k], recv_sem=rsem.at[k], device_id=to, device_id_type=MESH
        )

    right, left = dev(zmod(z + 1), xl, c, t), dev(zmod(z - 1), xl, c, t)
    cross = dev(z, 1 - xl, c, t)
    twin = dev(z, xl, 1 - c, t)

    def send(src, dst, k, to):
        copy = rcopy(src, dst, k, to)
        copy.start()
        pending.append(copy)

    def recv(dst, k):
        rcopy(dst, dst, k, twin).wait_recv()

    locals_ = [0]

    def lcopy(src, dst):
        copy = pltpu.make_async_copy(src, dst, lsem.at[locals_[0]])
        locals_[0] += 1
        copy.start()
        return copy

    n_right, n_left = nz // 2, (nz - 1) // 2

    class Ring:
        def __init__(self, slot):
            self.slot = slot
            self.kr, self.kl = alloc(n_right), alloc(n_left)

        def start(self):
            mine = self.slot(z)
            send(mine, mine, self.kr, right)
            if n_left:
                send(mine, mine, self.kl, left)

        def step(self, i):
            came = []
            ref = self.slot(zmod(z - i))
            recv(ref, self.kr + i - 1)
            came.append(zmod(z - i))
            if i < n_right:
                send(ref, ref, self.kr + i, right)
            if i <= n_left:
                ref = self.slot(zmod(z + i))
                recv(ref, self.kl + i - 1)
                came.append(zmod(z + i))
                if i < n_left:
                    send(ref, ref, self.kl + i, left)
            return came

    inner_copy = lcopy(inner, r["inner_v"])
    outer_copies = [
        lcopy(outer.at[:, pl.ds(pl.multiple_of((tt * 4 + s4) * chunk, chunk), chunk)], r["outer_v"].at[tt])
        for tt in range(nt)
    ]

    barrier = pltpu.get_barrier_semaphore()
    peers = [dev(z, xl, c, to_t(d)) for d in range(1, nt)]
    peers += [dev(z, *near(k), t) for k in range(1, 4)] + [right, left]
    for peer in peers:
        pl.semaphore_signal(barrier, inc=1, device_id=peer, device_id_type=MESH)
    pl.semaphore_wait(barrier, len(peers))

    pall, a_ref, wg, d_out = r["pall"], r["a"], r["wg"], r["d_out"]
    k_patch = alloc(nt)
    for d in range(1, nt):
        send(patches, pall.at[t], k_patch + d, dev(z, xl, c, to_t(d)))
    k_text = alloc(4)
    for k in range(1, 4):
        xx, cc = near(k)
        part = text.at[:, :, pl.ds(pl.multiple_of((xx * 2 + cc) * chunk, chunk), chunk)]
        send(part, a_ref.at[t, pl.ds(2 * xl, 2), c], k_text + k, dev(z, xx, cc, t))
    w_own = wg.at[pl.ds(pl.multiple_of(z * 256, 256), 256)]
    own_copies = [
        lcopy(patches, pall.at[t]),
        lcopy(
            text.at[:, :, pl.ds(pl.multiple_of(s4 * chunk, chunk), chunk)], a_ref.at[t, pl.ds(2 * xl, 2), c]
        ),
        lcopy(w, w_own),
        lcopy(cot.at[c], d_out.at[c]),
    ]
    k_cot = alloc(1)
    send(cot.at[1 - c], d_out.at[c], k_cot, twin)
    for copy in own_copies:
        copy.wait()
    ring_w = Ring(lambda zz: wg.at[pl.ds(pl.multiple_of(zz * 256, 256), 256)])
    ring_w.start()

    pick, place, mask = r["pick"], r["place"], r["mask"]
    total = nz * images
    pick[...] = jnp.where(
        r["grow"][...] == z * images + lax.broadcasted_iota(jnp.int32, (images, total), 0), 1.0, 0.0
    ).astype(BF)
    stands = jnp.where(
        r["krow"][...] == z * plane + lax.broadcasted_iota(jnp.int32, (plane, total), 0), 1.0, 0.0
    ).astype(BF)
    place[...] = dot_nt(stands, pick[...]).astype(BF)
    mask[...] = dot_nn(place[...], jnp.ones((images, chunk), BF))

    for k in range(1, 4):
        xx, cc = near(k)
        recv(a_ref.at[t, pl.ds(2 * xx, 2), cc], k_text + k)
    k_a = alloc(nt)
    for d in range(1, nt):
        send(a_ref.at[t], a_ref.at[t], k_a + d, dev(z, xl, c, to_t(d)))

    for d in range(1, nt):
        recv(pall.at[from_t(d)], k_patch + d)
    inner_copy.wait()
    vit = gain.shape[1]
    per = vit // pw
    hidden = None
    for piece in range(nt // per):
        wide = jnp.concatenate([pall[piece * per + i] for i in range(per)], axis=1).astype(F32)
        centre = jnp.mean(wide, axis=1, keepdims=True)
        shifted = wide - centre
        spread = jnp.mean(shifted * shifted, axis=1, keepdims=True)
        normed = (shifted * lax.rsqrt(spread + 1e-06) * gain[...] + bias[...]).astype(BF)
        term = dot_nn(normed, r["inner_v"][piece * vit : (piece + 1) * vit, :])
        hidden = term if hidden is None else hidden + term
    hidden = (0.5 * hidden * (1.0 + lax.erf(hidden * math.sqrt(0.5)))).astype(BF)

    def gather_sec(buf, own_value, n, extra=None):
        def block(zz, cc):
            return buf.at[cc, :, pl.ds(pl.multiple_of(zz * n, n), n), :]

        def half(xx):
            return buf.at[c, xx, pl.ds(pl.multiple_of(z * n, n), n), :]

        buf[c, xl, pl.ds(pl.multiple_of(z * n, n), n), :] = own_value
        k_cross, k_twin = alloc(1), alloc(nz)
        send(half(xl), half(xl), k_cross, cross)
        recv(half(1 - xl), k_cross)
        ring = Ring(lambda zz: block(zz, c))
        ring.start()
        send(block(z, c), block(z, c), k_twin, twin)
        done = [z]
        for i in range(1, n_right + 1):
            for zz in ring.step(i):
                send(block(zz, c), block(zz, c), k_twin + len(done), twin)
                done.append(zz)
            if extra is not None:
                extra(i)
        for j, zz in enumerate(done):
            recv(block(zz, 1 - c), k_twin + j)

    hall = r["hall"]
    if n_right > 1:
        ring_w.step(1)
    gather_sec(hall, hidden, rows)
    if n_right > 2:
        ring_w.step(2)

    hp = dot_nn(pick[...], hall[...].reshape(total, hall.shape[3])).astype(BF)
    for copy in outer_copies:
        copy.wait()
    part_s, part_r, img = r["part_s"], r["part_r"], r["img"]
    k_part, k_img = alloc(nt), alloc(nt)
    for d in range(1, nt):
        part_s[d] = dot_nn(hp, r["outer_v"][to_t(d)]).astype(BF)
        send(part_s.at[d], part_r.at[d], k_part + d, dev(z, xl, c, to_t(d)))
    mine = dot_nn(hp, r["outer_v"][t])
    for d in range(1, nt):
        recv(part_r.at[d], k_part + d)
        mine = mine + part_r[d].astype(F32)
    img[t] = mine.astype(BF)
    for d in range(1, nt):
        send(img.at[t], img.at[t], k_img + d, dev(z, xl, c, to_t(d)))
    if n_right > 3:
        ring_w.step(3)

    xf, ss = r["xf"], r["ss"]

    def take(tt):
        placed = dot_nn(place[...], img[tt])
        x = jnp.where(mask[...] > 0.5, placed, a_ref[tt].reshape(plane, chunk).astype(F32))
        xf[:, pl.ds(pl.multiple_of(tt * chunk, chunk), chunk)] = x.astype(BF)
        x = x * x
        return x[:, :128] + x[:, 128:]

    ss[...] = take(t)

    def take_next(d, carry):
        recv(a_ref.at[from_t(d)], k_a + d)
        recv(img.at[from_t(d)], k_img + d)
        ss[...] += take(from_t(d))
        return carry

    lax.fori_loop(1, nt, take_next, 0)
    ss_all, inv = r["ss_all"], r["inv"]
    squares = jnp.sum(ss[...], axis=1, keepdims=True)
    for o in range(4):
        ss_all[s4, o] = row_tile(squares[o * 128 : (o + 1) * 128])
    k_ss, k_c = alloc(4), alloc(4)
    for k in range(1, 4):
        send(ss_all.at[s4], ss_all.at[s4], k_ss + k, dev(z, *near(k), t))
    ring_w.step(n_right)

    c_s, c_r, cn = r["c_s"], r["c_r"], r["cn"]
    for k in (3, 2, 1, 0):
        xx, cc = near(k)
        o = xx * 2 + cc
        c_o = dot_nn(xf[pl.ds(pl.multiple_of(o * 128, 128), 128), :], wg[...])
        if k:
            c_s[k] = c_o.astype(BF)
            send(c_s.at[k], c_r.at[k], k_c + k, dev(z, xx, cc, t))
        else:
            cn[...] = c_o
    for k in range(1, 4):
        xx, cc = near(k)
        recv(ss_all.at[xx * 2 + cc], k_ss + k)
    for o in range(4):
        tile = ss_all[0, o] + ss_all[1, o] + ss_all[2, o] + ss_all[3, o]
        inv[o] = column_of(lax.rsqrt(tile / width + 1e-06))
    projected = cn[...]
    for k in range(1, 4):
        recv(c_r.at[k], k_c + k)
        projected = projected + c_r[k].astype(F32)
    projected = projected * inv[s4][:, :1]
    cn[...] = projected
    heads = (projected.shape[1] - 2 * HEAD_DIM) // HEAD_DIM
    qs, kv, dos = r["qs"], r["kv"], r["dos"]
    for h in range(heads):
        qs[h] = projected[:, h * 128 : (h + 1) * 128].astype(BF)
    kv[z, xl] = projected[:, heads * 128 :].astype(BF)

    k_kv = alloc(1)
    send(kv.at[z, xl], kv.at[z, xl], k_kv, cross)
    recv(kv.at[z, 1 - xl], k_kv)
    ring_kv = Ring(lambda zz: kv.at[zz])
    ring_kv.start()
    recv(d_out.at[1 - c], k_cot)
    for h in range(heads):
        dos[h] = d_out[:, :, h * 128 : (h + 1) * 128].reshape(128, 128)
    for i in range(1, n_right + 1):
        ring_kv.step(i)

    ph, ds, att, dq = r["ph"], r["ds"], r["att"], r["dq"]

    def head(h, carry):
        keys = kv[:, :, :, :128].reshape(seq, 128)
        values = kv[:, :, :, 128:].reshape(seq, 128)
        scores = dot_nt(qs[h], keys) * scale
        query_pos = z * 256 + xl * 128 + lax.broadcasted_iota(jnp.int32, (128, seq), 0)
        scores = jnp.where(lax.broadcasted_iota(jnp.int32, (128, seq), 1) <= query_pos, scores, -1e30)
        raw = jnp.exp(scores - jnp.max(scores, axis=1, keepdims=True))
        probs = raw / jnp.sum(raw, axis=1, keepdims=True)
        half = probs.astype(BF)
        ph[h] = half
        att[h] = dot_nn(half, values).astype(BF)
        grad_probs = dot_nt(dos[h], values)
        delta = jnp.sum(probs * grad_probs, axis=1, keepdims=True)
        grad = (probs * (grad_probs - delta)).astype(BF)
        ds[h] = grad
        dq[h] = (dot_nn(grad, keys) * scale).astype(BF)
        return carry

    lax.fori_loop(0, heads, head, 0)
    att_o, att_r = r["att_o"], r["att_r"]
    for h in range(heads):
        att_o[:, :, h * 128 : (h + 1) * 128] = att[h].reshape(2, 64, 128)
    k_att = alloc(1)
    send(att_o.at[1 - c], att_r, k_att, twin)

    dkv = r["dkv"]

    def key_block(zz, carry):
        lanes = pl.ds(pl.multiple_of(zz * 256, 256), 256)
        dkv[zz, :, :128] = dot_tn(ds[:, :, lanes].reshape(heads * 128, 256), qs[...].reshape(heads * 128, 128))
        dkv[zz, :, 128:] = dot_tn(ph[:, :, lanes].reshape(heads * 128, 256), dos[...].reshape(heads * 128, 128))
        return carry

    lax.fori_loop(0, nz, key_block, 0)

    sr, rr, sl, rl = r["sr"], r["rr"], r["sl"], r["rl"]
    kr, kl = alloc(n_right), alloc(max(n_left, 1))
    for i in range(n_right + 1):
        value = dkv[zmod(z + n_right - i)]
        if i:
            recv(rr.at[i - 1], kr + i - 1)
            value = value + rr[i - 1].astype(F32)
        if i < n_right:
            sr[i] = value.astype(BF)
            send(sr.at[i], rr.at[i], kr + i, right)
        else:
            dkv[z] = value
        if n_left and i < n_left:
            value = dkv[zmod(z - n_left + i)]
            if i:
                recv(rl.at[i - 1], kl + i - 1)
                value = value + rl[i - 1].astype(F32)
            sl[i] = value.astype(BF)
            send(sl.at[i], rl.at[i], kl + i, left)
    if n_left:
        recv(rl.at[n_left - 1], kl + n_left - 1)
        dkv[z] += rl[n_left - 1].astype(F32)
    dx_s, dx_r = r["dx_s"], r["dx_r"]
    k_dx = alloc(1)
    dx_s[...] = dkv[z, pl.ds(pl.multiple_of((1 - xl) * 128, 128), 128), :].astype(BF)
    send(dx_s, dx_r, k_dx, cross)
    recv(dx_r, k_dx)
    grad_kv = dkv[z, pl.ds(pl.multiple_of(xl * 128, 128), 128), :] + dx_r[...].astype(F32)

    gg, inn, int_all = r["gg"], r["inn"], r["int_all"]
    pieces = [dq[h] for h in range(heads)]
    pieces += [(grad_kv[:, :128] * scale).astype(BF), grad_kv[:, 128:].astype(BF)]
    grads = jnp.concatenate(pieces, axis=1)
    gg[s4] = grads
    inn[s4] = row_tile(jnp.sum(grads.astype(F32) * cn[...], axis=1, keepdims=True))
    k_gg, k_inn = alloc(4), alloc(4)
    for k in range(1, 4):
        to = dev(z, *near(k), t)
        send(gg.at[s4], gg.at[s4], k_gg + k, to)
        send(inn.at[s4], inn.at[s4], k_inn + k, to)
    for k in range(1, 4):
        xx, cc = near(k)
        recv(gg.at[xx * 2 + cc], k_gg + k)
        recv(inn.at[xx * 2 + cc], k_inn + k)
    int_all[t] = inn[...]
    k_int, k_back = alloc(nt), alloc(nt)
    for d in range(1, nt):
        send(int_all.at[t], int_all.at[t], k_int + d, dev(z, xl, c, to_t(d)))

    bs, br, bo = r["bs"], r["br"], r["bo"]

    def back(d, carry):
        tt = to_t(d)
        block = dot_nt(
            gg[...].reshape(plane, gg.shape[2]), wg[pl.ds(pl.multiple_of(tt * chunk, chunk), chunk), :]
        )
        bs[d] = block.astype(BF)
        rcopy(bs.at[d], br.at[d], k_back + d, dev(z, xl, c, tt)).start()
        return carry

    lax.fori_loop(1, nt, back, 0)
    for d in range(1, nt):
        pending.append(rcopy(bs.at[d], br.at[d], k_back + d, dev(z, xl, c, to_t(d))))
    bo[...] = dot_nt(gg[...].reshape(plane, gg.shape[2]), wg[pl.ds(pl.multiple_of(t * chunk, chunk), chunk), :])
    for d in range(1, nt):
        recv(int_all.at[from_t(d)], k_int + d)
    for d in range(1, nt):
        recv(br.at[d], k_back + d)
        bo[...] += br[d].astype(F32)
    gi, gt_s, gt_r = r["gi"], r["gt_s"], r["gt_r"]
    for o in range(4):
        tile = int_all[0, o]
        for d in range(1, nt):
            tile = tile + int_all[d, o]
        inv_o = inv[o][:, :1]
        span = slice(o * 128, (o + 1) * 128)
        x = xf[span, pl.ds(pl.multiple_of(t * chunk, chunk), chunk)].astype(F32)
        grad = (inv_o * bo[span, :] - x * (inv_o * inv_o * column_of(tile)[:, :1] / width)).astype(BF)
        gi[span, :] = grad
        gt_s[o] = jnp.where(mask[span, :] > 0.5, jnp.zeros_like(grad), grad).reshape(2, 64, chunk)

    k_gt = alloc(4)
    for k in range(1, 4):
        xx, cc = near(k)
        send(gt_s.at[pl.ds(2 * xx, 2), cc], gt_r.at[s4], k_gt + k, dev(z, xx, cc, t))
    rall = r["rall"]
    gather_sec(rall, dot_tn(place[...], gi[...]).astype(BF), images)
    wanted = jnp.where(r["gcol"][...] == lax.broadcasted_iota(jnp.int32, (rows, total), 1), 1.0, 0.0).astype(BF)
    for xx in range(2):
        for cc in range(2):
            o = xx * 2 + cc
            r["gimage"][:, o * chunk : (o + 1) * chunk] = dot_nn(wanted, rall[cc, xx]).astype(BF)

    gt_r[s4] = gt_s[pl.ds(2 * xl, 2), c]
    for k in range(1, 4):
        xx, cc = near(k)
        recv(gt_r.at[xx * 2 + cc], k_gt + k)
    for o in range(4):
        r["gtext"][:, :, o * chunk : (o + 1) * chunk] = gt_r[o]
    recv(att_r, k_att)
    r["attended"][c] = att_o[c]
    r["attended"][1 - c] = att_r[...]
    for copy in pending:
        copy.wait_send()


def per_device(
    patches,
    merge_gain,
    merge_bias,
    merge_inner,
    merge_outer,
    slot_target,
    text_embed,
    norm_gain,
    query_weight,
    key_weight,
    value_weight,
    attn_cotangent,
):
    nsec, nt = lax.axis_size("sec"), lax.axis_size("tp")
    nz, ny = nsec // 4, max(nt // 2, 1)
    sec = lax.axis_index("sec")
    rows, pw = patches.shape
    hid = merge_inner.shape[1]
    micro, tok, feat = text_embed.shape
    chunk = feat // 4
    seq = tok * nsec
    images = 4 * rows
    total = nz * images
    depth = query_weight.shape[0]
    heads = query_weight.shape[1] // HEAD_DIM
    cols = (heads + 2) * HEAD_DIM
    plane = 512

    batch, pos = slot_target // seq, slot_target % seq
    key = (pos // 256) * plane + (pos // 128 % 2) * 256 + batch * 128 + pos % 128
    rank = jnp.sum((key[None, :] < key[:, None]).astype(jnp.int32), axis=1)

    def row_order(v):
        return v.reshape(nz, 2, 2, rows).transpose(2, 1, 0, 3).reshape(1, total)

    gcol = lax.dynamic_slice_in_dim(rank, sec * rows, rows).reshape(rows, 1)
    my_gain = lax.dynamic_slice_in_dim(norm_gain, sec * depth, depth)[:, None]
    weight = jnp.concatenate([query_weight, key_weight, value_weight], axis=1)
    weight = (weight.astype(F32) * my_gain).astype(BF)

    vmem, anyspace = pl.BlockSpec(memory_space=pltpu.VMEM), pl.BlockSpec(memory_space=pl.ANY)
    n_right, n_left = nz // 2, max((nz - 1) // 2, 1)
    n_sem = 192
    ins = ["patches", "gain", "bias", "inner", "outer", "krow", "grow", "gcol", "text", "w", "cot"]
    outs = ["attended", "gtext", "gimage"]
    scratch = dict(
        pall=((nt, rows, pw), BF),
        inner_v=(merge_inner.shape, BF),
        outer_v=((nt, hid, chunk), BF),
        a=((nt, 4, 2, tok, chunk), BF),
        wg=((nz * depth, cols), BF),
        d_out=((2, tok, heads * HEAD_DIM), BF),
        hall=((2, 2, nz * rows, hid), BF),
        pick=((images, total), BF),
        place=((plane, images), BF),
        mask=((plane, chunk), F32),
        part_s=((nt, images, chunk), BF),
        part_r=((nt, images, chunk), BF),
        img=((nt, images, chunk), BF),
        xf=((plane, nt * chunk), BF),
        ss=((plane, 128), F32),
        ss_all=((4, 4, 8, 128), F32),
        inv=((4, 128, 128), F32),
        c_s=((4, 128, cols), BF),
        c_r=((4, 128, cols), BF),
        cn=((128, cols), F32),
        qs=((heads, 128, 128), BF),
        kv=((nz, 2, 128, 256), BF),
        dos=((heads, 128, 128), BF),
        ph=((heads, 128, seq), BF),
        ds=((heads, 128, seq), BF),
        att=((heads, 128, 128), BF),
        dq=((heads, 128, 128), BF),
        att_o=((2, tok, heads * HEAD_DIM), BF),
        att_r=((tok, heads * HEAD_DIM), BF),
        dkv=((nz, 256, 256), F32),
        sr=((n_right, 256, 256), BF),
        rr=((n_right, 256, 256), BF),
        sl=((n_left, 256, 256), BF),
        rl=((n_left, 256, 256), BF),
        dx_s=((128, 256), BF),
        dx_r=((128, 256), BF),
        gg=((4, 128, cols), BF),
        inn=((4, 8, 128), F32),
        int_all=((nt, 4, 8, 128), F32),
        bs=((nt, plane, chunk), BF),
        br=((nt, plane, chunk), BF),
        bo=((plane, chunk), F32),
        gi=((plane, chunk), BF),
        gt_s=((4, 2, tok, chunk), BF),
        gt_r=((4, 2, tok, chunk), BF),
        rall=((2, 2, nz * images, chunk), BF),
    )
    names = ins + outs + list(scratch) + ["ssem", "rsem", "lsem", "n_sem"]
    call = pl.pallas_call(
        lambda *refs: kernel(nz, nt, ny, names, *refs, n_sem),
        out_shape=(
            jax.ShapeDtypeStruct((micro, tok, heads * HEAD_DIM), BF),
            jax.ShapeDtypeStruct((micro, tok, feat), BF),
            jax.ShapeDtypeStruct((rows, feat), BF),
        ),
        in_specs=[anyspace if n in ("inner", "outer") else vmem for n in ins],
        out_specs=(vmem,) * 3,
        scratch_shapes=[pltpu.VMEM(shape, dtype) for shape, dtype in scratch.values()]
        + [
            pltpu.SemaphoreType.DMA((n_sem,)),
            pltpu.SemaphoreType.DMA((n_sem,)),
            pltpu.SemaphoreType.DMA((16,)),
        ],
        compiler_params=pltpu.CompilerParams(
            collective_id=0, has_side_effects=True, vmem_limit_bytes=56 * 1024 * 1024
        ),
        name="merged_step",
    )
    return call(
        patches,
        merge_gain.reshape(1, -1),
        merge_bias.reshape(1, -1),
        merge_inner,
        merge_outer,
        row_order(key),
        row_order(rank),
        gcol,
        text_embed,
        weight,
        attn_cotangent,
    )


def solution(mesh):
    return jax.shard_map(
        per_device,
        mesh=mesh,
        in_specs=(
            P("sec", "tp"),
            P(),
            P(),
            P(None, "tp"),
            P("tp", None),
            P(),
            P(None, "sec", "tp"),
            P(),
            P("sec", "tp"),
            P("sec", "tp"),
            P("sec", "tp"),
            P(None, "sec", "tp"),
        ),
        out_specs=(P(None, "sec", "tp"), P(None, "sec", "tp"), P("sec", "tp")),
        check_vma=False,
    )
```

```python
import functools
import math

import jax
import jax.numpy as jnp
from jax import lax
from jax.experimental import pallas as pl
from jax.experimental.pallas import tpu as pltpu
from jax.sharding import PartitionSpec as P

HEAD_DIM = 128
BF = jnp.bfloat16
F32 = jnp.float32
MESH = pl.DeviceIdType.MESH
TEXT_AT = 2
W_AT = 2


def dot_nn(a, b):
    return jnp.dot(a, b, preferred_element_type=F32)


def dot_nt(a, b):
    return lax.dot_general(a, b, (((1,), (1,)), ((), ())), preferred_element_type=F32)


def dot_tn(a, b):
    return lax.dot_general(a, b, (((0,), (0,)), ((), ())), preferred_element_type=F32)


def row_tile(column):
    return jnp.broadcast_to(column, (128, 128)).T[:8]


def column_of(tile):
    return jnp.broadcast_to(tile[0:1, :], (128, 128)).T


def kernel(nz, nt, ny, names, *refs):
    r = dict(zip(names, refs))
    patches, gain, bias, inner, outer = (r[n] for n in ("patches", "gain", "bias", "inner", "outer"))
    text, cot = r["text"], r["cot"]
    ssem, rsem, lsem = r["ssem"], r["rsem"], r["lsem"]
    sec, t = lax.axis_index("sec"), lax.axis_index("tp")
    z, s4 = lax.div(sec, 4), lax.rem(sec, 4)
    xl, c = lax.div(s4, 2), lax.rem(s4, 2)
    nxh = nt // ny
    xh, y = lax.div(t, ny), lax.rem(t, ny)
    rows, pw = patches.shape
    chunk = text.shape[2] // 4
    plane = 4 * 128
    images = 4 * rows
    width = text.shape[2] * nt
    seq = nz * 256
    scale = 1.0 / math.sqrt(HEAD_DIM)

    def zmod(v):
        return lax.rem(v + nz, nz)

    def to_t(d):
        dx, dy = d // ny, d % ny
        return lax.rem(xh + dx, nxh) * ny + lax.rem(y + dy, ny)

    def from_t(d):
        dx, dy = d // ny, d % ny
        return lax.rem(xh + nxh - dx, nxh) * ny + lax.rem(y + ny - dy, ny)

    def near(k):
        a = 1 - xl if k // 2 else xl
        b = 1 - c if k % 2 else c
        return a, b

    def dev(zz, xx, cc, tt):
        return (zz * 4 + xx * 2 + cc, tt)

    counter = [0]
    pending = []

    def alloc(n):
        first = counter[0]
        counter[0] += n
        assert counter[0] <= r["n_sem"]
        return first

    def rcopy(src, dst, k, to):
        return pltpu.make_async_remote_copy(
            src_ref=src, dst_ref=dst, send_sem=ssem.at[k], recv_sem=rsem.at[k], device_id=to, device_id_type=MESH
        )

    right, left = dev(zmod(z + 1), xl, c, t), dev(zmod(z - 1), xl, c, t)
    cross = dev(z, 1 - xl, c, t)
    twin = dev(z, xl, 1 - c, t)

    def send(src, dst, k, to):
        copy = rcopy(src, dst, k, to)
        copy.start()
        pending.append(copy)

    def recv(dst, k):
        rcopy(dst, dst, k, twin).wait_recv()

    locals_ = [0]

    def lcopy(src, dst):
        copy = pltpu.make_async_copy(src, dst, lsem.at[locals_[0]])
        locals_[0] += 1
        copy.start()
        return copy

    n_right, n_left = nz // 2, (nz - 1) // 2

    class Ring:
        def __init__(self, slot):
            self.slot = slot
            self.kr, self.kl = alloc(n_right), alloc(n_left)

        def start(self):
            mine = self.slot(z)
            send(mine, mine, self.kr, right)
            if n_left:
                send(mine, mine, self.kl, left)

        def step(self, i):
            came = []
            ref = self.slot(zmod(z - i))
            recv(ref, self.kr + i - 1)
            came.append(zmod(z - i))
            if i < n_right:
                send(ref, ref, self.kr + i, right)
            if i <= n_left:
                ref = self.slot(zmod(z + i))
                recv(ref, self.kl + i - 1)
                came.append(zmod(z + i))
                if i < n_left:
                    send(ref, ref, self.kl + i, left)
            return came

    pall, a_ref, wg, d_out, w_v = r["pall"], r["a"], r["wg"], r["d_out"], r["w_v"]
    own_copies = [
        lcopy(patches, pall.at[t]),
        lcopy(
            text.at[:, :, pl.ds(pl.multiple_of(s4 * chunk, chunk), chunk)], a_ref.at[t, pl.ds(2 * xl, 2), c]
        ),
        lcopy(cot.at[c], d_out.at[c]),
    ]
    w_copies = []
    first = 0
    for name in ("wq", "wk", "wv"):
        n = r[name].shape[1]
        w_copies.append(lcopy(r[name], w_v.at[:, pl.ds(first, n)]))
        first += n
    inner_copy = lcopy(inner, r["inner_v"])
    outer_copies = [
        lcopy(outer.at[:, pl.ds(pl.multiple_of((tt * 4 + s4) * chunk, chunk), chunk)], r["outer_v"].at[tt])
        for tt in range(nt)
    ]

    barrier = pltpu.get_barrier_semaphore()
    peers = [dev(z, xl, c, to_t(d)) for d in range(1, nt)]
    peers += [dev(z, *near(k), t) for k in range(1, 4)] + [right, left]
    for peer in peers:
        pl.semaphore_signal(barrier, inc=1, device_id=peer, device_id_type=MESH)
    pl.semaphore_wait(barrier, len(peers))

    k_patch = alloc(nt)
    for d in range(1, nt):
        send(patches, pall.at[t], k_patch + d, dev(z, xl, c, to_t(d)))
    k_text = alloc(4)
    for k in range(1, 4):
        xx, cc = near(k)
        part = text.at[:, :, pl.ds(pl.multiple_of((xx * 2 + cc) * chunk, chunk), chunk)]
        send(part, a_ref.at[t, pl.ds(2 * xl, 2), c], k_text + k, dev(z, xx, cc, t))
    k_cot = alloc(1)
    send(cot.at[1 - c], d_out.at[c], k_cot, twin)

    r["gain_v"][...] = r["ngain"][...].reshape(r["gain_v"].shape)
    for copy in w_copies:
        copy.wait()
    for i in range(2):
        factor = column_of(r["gain_v"][pl.ds(sec * 2 + i, 1), :])[:, :1]
        rows_i = pl.ds(pl.multiple_of(z * 256 + i * 128, 128), 128)
        wg[rows_i, :] = (w_v[i * 128 : (i + 1) * 128, :].astype(F32) * factor).astype(BF)
    ring_w = Ring(lambda zz: wg.at[pl.ds(pl.multiple_of(zz * 256, 256), 256)])
    ring_w.start()

    pick, place, mask, kcol = r["pick"], r["place"], r["mask"], r["kcol"]
    total = nz * images
    slot = r["slot"][...].reshape(1, total)
    bits = seq.bit_length() - 1
    batch, pos = slot >> bits, slot & (seq - 1)
    key = ((pos >> 8) * plane + ((pos >> 7) & 1) * 256 + batch * 128 + (pos & 127)).astype(F32)
    for i in range(total // 128):
        kcol[i * 128 : (i + 1) * 128, :] = column_of(key[:, i * 128 : (i + 1) * 128])
    rank = jnp.sum(jnp.where(kcol[...][:, :1] < key, 1.0, 0.0), axis=0, keepdims=True)
    wide_rows = lax.broadcasted_iota(jnp.int32, (images, total), 0) + z * images
    pick[...] = jnp.where(rank == wide_rows.astype(F32), 1.0, 0.0).astype(BF)
    wide_rows = lax.broadcasted_iota(jnp.int32, (plane, total), 0) + z * plane
    stands = jnp.where(key == wide_rows.astype(F32), 1.0, 0.0).astype(BF)
    place[...] = dot_nt(stands, pick[...]).astype(BF)
    mask[...] = dot_nn(place[...], jnp.ones((images, chunk), BF))
    own_key = kcol[pl.ds(pl.multiple_of(z * images, images), images), :][:, :1]
    own_rank = jnp.sum(jnp.where(key < own_key, 1.0, 0.0), axis=1, keepdims=True)
    wanted, tsel, isel = r["wanted"], r["tsel"], r["isel"]
    wanted[...] = jnp.where(
        own_rank == lax.broadcasted_iota(jnp.int32, (images, total), 1).astype(F32), 1.0, 0.0
    ).astype(BF)
    earlier = jnp.where(
        lax.broadcasted_iota(jnp.int32, (128, 128), 0) < lax.broadcasted_iota(jnp.int32, (128, 128), 1), 1.0, 0.0
    ).astype(BF)

    def select(flags, count):
        nth = dot_nn(flags[:8].astype(BF), earlier)[:1]
        return jnp.where(
            nth == lax.broadcasted_iota(jnp.int32, (count, 128), 0).astype(F32), flags[:1], 0.0
        ).astype(BF)

    texts = 128 - rows
    for o in range(4):
        tsel[o] = select(1.0 - mask[o * 128 : (o + 1) * 128, :128].T, texts)
    isel[...] = select(mask[pl.ds(pl.multiple_of(s4 * 128, 128), 128), :128].T, rows)

    for copy in own_copies:
        copy.wait()

    for k in range(1, 4):
        xx, cc = near(k)
        recv(a_ref.at[t, pl.ds(2 * xx, 2), cc], k_text + k)
    k_a = alloc(nt)

    def text_out():
        for d in range(1, nt):
            send(a_ref.at[t], a_ref.at[t], k_a + d, dev(z, xl, c, to_t(d)))

    if TEXT_AT == 0:
        text_out()
    for d in range(1, nt):
        recv(pall.at[from_t(d)], k_patch + d)
    if TEXT_AT == 1:
        text_out()
    if W_AT == 1:
        ring_w.step(1)
    inner_copy.wait()
    vit = gain.shape[0]
    per = vit // pw
    hidden = None
    for piece in range(nt // per):
        wide = jnp.concatenate([pall[piece * per + i] for i in range(per)], axis=1).astype(F32)
        centre = jnp.mean(wide, axis=1, keepdims=True)
        shifted = wide - centre
        spread = jnp.mean(shifted * shifted, axis=1, keepdims=True)
        normed = (shifted * lax.rsqrt(spread + 1e-06) * gain[...].reshape(1, vit) + bias[...].reshape(1, vit)).astype(BF)
        term = dot_nn(normed, r["inner_v"][piece * vit : (piece + 1) * vit, :])
        hidden = term if hidden is None else hidden + term
    hidden = (0.5 * hidden * (1.0 + lax.erf(hidden * math.sqrt(0.5)))).astype(BF)

    class Gather:
        def __init__(self, slot_of):
            self.slot_of = slot_of
            self.k_cross, self.k_twin = alloc(1), alloc(2 * nz)
            mine = slot_of(z, xl, c)
            send(mine, mine, self.k_cross, cross)
            self.rings = [Ring(lambda zz: slot_of(zz, xl, c)), Ring(lambda zz: slot_of(zz, 1 - xl, c))]
            self.done = []
            self.rings[0].start()
            self.arrived(z, xl)

        def arrived(self, zz, xx):
            ref = self.slot_of(zz, xx, c)
            send(ref, ref, self.k_twin + len(self.done), twin)
            self.done.append((zz, xx))

        def crossed(self):
            recv(self.slot_of(z, 1 - xl, c), self.k_cross)
            self.rings[1].start()
            self.arrived(z, 1 - xl)

        def step(self, i):
            for ring, xx in zip(self.rings, (xl, 1 - xl)):
                for zz in ring.step(i):
                    self.arrived(zz, xx)

        def finish(self):
            for j, (zz, xx) in enumerate(self.done):
                recv(self.slot_of(zz, xx, 1 - c), self.k_twin + j)

    hall = r["hall"]
    hall[z, xl, c] = hidden
    if W_AT == 2:
        ring_w.step(1)
    gather = Gather(lambda zz, xx, cc: hall.at[zz, xx, cc])
    gather.crossed()
    if TEXT_AT == 2:
        text_out()
    for i in range(1, n_right + 1):
        gather.step(i)
    gather.finish()
    if n_right > 2:
        ring_w.step(2)
    if TEXT_AT == 3:
        text_out()

    hp = dot_nn(pick[...], hall[...].reshape(total, hall.shape[4])).astype(BF)
    for copy in outer_copies:
        copy.wait()
    part_s, part_r, img = r["part_s"], r["part_r"], r["img"]
    k_part, k_img = alloc(nt), alloc(nt)
    for d in range(1, nt):
        part_s[d] = dot_nn(hp, r["outer_v"][to_t(d)]).astype(BF)
        send(part_s.at[d], part_r.at[d], k_part + d, dev(z, xl, c, to_t(d)))
    mine = dot_nn(hp, r["outer_v"][t])
    for d in range(1, nt):
        recv(part_r.at[d], k_part + d)
        mine = mine + part_r[d].astype(F32)
    img[t] = mine.astype(BF)
    for d in range(1, nt):
        send(img.at[t], img.at[t], k_img + d, dev(z, xl, c, to_t(d)))
    if n_right > 3:
        ring_w.step(3)

    xf, ss = r["xf"], r["ss"]

    def take(tt):
        placed = dot_nn(place[...], img[tt])
        x = jnp.where(mask[...] > 0.5, placed, a_ref[tt].reshape(plane, chunk).astype(F32))
        xf[:, pl.ds(pl.multiple_of(tt * chunk, chunk), chunk)] = x.astype(BF)
        x = x * x
        return x[:, :128] + x[:, 128:]

    ss[...] = take(t)

    def take_next(d, carry):
        recv(a_ref.at[from_t(d)], k_a + d)
        recv(img.at[from_t(d)], k_img + d)
        ss[...] += take(from_t(d))
        return carry

    lax.fori_loop(1, nt, take_next, 0)
    ss_all, inv = r["ss_all"], r["inv"]
    squares = jnp.sum(ss[...], axis=1, keepdims=True)
    for o in range(4):
        ss_all[s4, o] = row_tile(squares[o * 128 : (o + 1) * 128])
    k_ss, k_c = alloc(4), alloc(4)
    for k in range(1, 4):
        send(ss_all.at[s4], ss_all.at[s4], k_ss + k, dev(z, *near(k), t))
    ring_w.step(n_right)

    c_s, c_r, cn = r["c_s"], r["c_r"], r["cn"]
    def project(xx, cc):
        return dot_nn(xf[pl.ds(pl.multiple_of((xx * 2 + cc) * 128, 128), 128), :], wg[...])

    c_s[0] = project(1 - xl, 1 - c).astype(BF)
    send(c_s.at[0], c_r.at[0], k_c, twin)
    c_s[1] = project(xl, 1 - c).astype(BF)
    send(c_s.at[1], c_r.at[1], k_c + 1, twin)
    other = project(1 - xl, c)
    recv(c_r.at[0], k_c)
    c_s[2] = (other + c_r[0].astype(F32)).astype(BF)
    send(c_s.at[2], c_r.at[2], k_c + 2, cross)
    cn[...] = project(xl, c)
    for k in range(1, 4):
        xx, cc = near(k)
        recv(ss_all.at[xx * 2 + cc], k_ss + k)
    for o in range(4):
        tile = ss_all[0, o] + ss_all[1, o] + ss_all[2, o] + ss_all[3, o]
        inv[o] = column_of(lax.rsqrt(tile / width + 1e-06))
    projected = cn[...]
    for k in range(1, 3):
        recv(c_r.at[k], k_c + k)
        projected = projected + c_r[k].astype(F32)
    projected = projected * inv[s4][:, :1]
    cn[...] = projected
    heads = (projected.shape[1] - 2 * HEAD_DIM) // HEAD_DIM
    qs, kv, dos = r["qs"], r["kv"], r["dos"]
    for h in range(heads):
        qs[h] = projected[:, h * 128 : (h + 1) * 128].astype(BF)
    kv[z, xl] = projected[:, heads * 128 :].astype(BF)

    k_kv = alloc(1)
    send(kv.at[z, xl], kv.at[z, xl], k_kv, cross)
    rings = [Ring(lambda zz: kv.at[zz, xl]), Ring(lambda zz: kv.at[zz, 1 - xl])]
    rings[0].start()
    recv(kv.at[z, 1 - xl], k_kv)
    rings[1].start()
    own_s, own_r = r["own_s"], r["own_r"]
    k_own = alloc(nt)
    h_own = hall[z].reshape(images, hall.shape[4])
    for d in range(1, nt):
        own_s[d] = dot_nn(h_own, r["outer_v"][to_t(d)]).astype(BF)
        send(own_s.at[d], own_r.at[d], k_own + d, dev(z, xl, c, to_t(d)))
    recv(d_out.at[1 - c], k_cot)
    for h in range(heads):
        dos[h] = d_out[:, :, h * 128 : (h + 1) * 128].reshape(128, 128)
    for i in range(1, n_right + 1):
        rings[0].step(i)
        rings[1].step(i)

    ph, ds, att, dq = r["ph"], r["ds"], r["att"], r["dq"]

    def head(h, carry):
        keys = kv[:, :, :, :128].reshape(seq, 128)
        values = kv[:, :, :, 128:].reshape(seq, 128)
        scores = dot_nt(qs[h], keys) * scale
        query_pos = z * 256 + xl * 128 + lax.broadcasted_iota(jnp.int32, (128, seq), 0)
        scores = jnp.where(lax.broadcasted_iota(jnp.int32, (128, seq), 1) <= query_pos, scores, -1e30)
        raw = jnp.exp(scores - jnp.max(scores, axis=1, keepdims=True))
        probs = raw / jnp.sum(raw, axis=1, keepdims=True)
        half = probs.astype(BF)
        ph[h] = half
        att[h] = dot_nn(half, values).astype(BF)
        grad_probs = dot_nt(dos[h], values)
        delta = jnp.sum(probs * grad_probs, axis=1, keepdims=True)
        grad = (probs * (grad_probs - delta)).astype(BF)
        ds[h] = grad
        dq[h] = (dot_nn(grad, keys) * scale).astype(BF)
        return carry

    lax.fori_loop(0, heads, head, 0)
    att_o, att_r = r["att_o"], r["att_r"]
    for h in range(heads):
        att_o[:, :, h * 128 : (h + 1) * 128] = att[h].reshape(2, 64, 128)
    k_att = alloc(1)
    send(att_o.at[1 - c], att_r, k_att, twin)

    dkv = r["dkv"]

    def key_block(zz, carry):
        lanes = pl.ds(pl.multiple_of(zz * 256, 256), 256)
        dkv[zz, :, :128] = dot_tn(ds[:, :, lanes].reshape(heads * 128, 256), qs[...].reshape(heads * 128, 128))
        dkv[zz, :, 128:] = dot_tn(ph[:, :, lanes].reshape(heads * 128, 256), dos[...].reshape(heads * 128, 128))
        return carry

    lax.fori_loop(0, nz, key_block, 0)

    sr, rr, sl, rl = r["sr"], r["rr"], r["sl"], r["rl"]
    kr, kl = alloc(2 * n_right), alloc(2 * max(n_left, 1))
    dx_s, dx_r = r["dx_s"], r["dx_r"]
    k_dx = alloc(1)

    def rows_of(xx):
        return pl.ds(pl.multiple_of(xx * 128, 128), 128)

    halves = ((0, 1 - xl), (1, xl))
    for i in range(n_right + 1):
        for half, xx in halves:
            value = dkv[zmod(z + n_right - i), rows_of(xx), :]
            if i:
                recv(rr.at[half, i - 1], kr + 2 * (i - 1) + half)
                value = value + rr[half, i - 1].astype(F32)
            if i < n_right:
                sr[half, i] = value.astype(BF)
                send(sr.at[half, i], rr.at[half, i], kr + 2 * i + half, right)
            elif half == 0:
                if n_left:
                    value = value + rl[half, n_left - 1].astype(F32)
                dx_s[...] = value.astype(BF)
                send(dx_s, dx_r, k_dx, cross)
            else:
                if n_left:
                    value = value + rl[half, n_left - 1].astype(F32)
                grad_kv = value
        for half, xx in halves:
            if n_left and i <= n_left:
                if i:
                    recv(rl.at[half, i - 1], kl + 2 * (i - 1) + half)
                if i < n_left:
                    value = dkv[zmod(z - n_left + i), rows_of(xx), :]
                    if i:
                        value = value + rl[half, i - 1].astype(F32)
                    sl[half, i] = value.astype(BF)
                    send(sl.at[half, i], rl.at[half, i], kl + 2 * i + half, left)
    recv(dx_r, k_dx)
    grad_kv = grad_kv + dx_r[...].astype(F32)

    gg, inn, int_all = r["gg"], r["inn"], r["int_all"]
    pieces = [dq[h] for h in range(heads)]
    pieces += [(grad_kv[:, :128] * scale).astype(BF), grad_kv[:, 128:].astype(BF)]
    grads = jnp.concatenate(pieces, axis=1)
    inn_tile = row_tile(jnp.sum(grads.astype(F32) * cn[...], axis=1, keepdims=True))
    inn[s4] = inn_tile
    marks = isel[...].astype(F32)
    beside = (
        jnp.sum(marks * inv[s4].T[:1], axis=1, keepdims=True),
        jnp.sum(marks * inn_tile[:1], axis=1, keepdims=True),
    )
    lane = lax.broadcasted_iota(jnp.int32, (rows, 128), 1)
    extra = jnp.zeros((rows, 128), F32)
    for n, value in enumerate(beside):
        for m in range(3):
            part = value.astype(BF).astype(F32)
            extra = jnp.where(lane == 3 * n + m, part, extra)
            value = value - part
    rall = r["rall"]
    rall[z, xl, c] = jnp.concatenate([dot_nn(isel[...], grads).astype(BF), extra.astype(BF)], axis=1)
    gather = Gather(lambda zz, xx, cc: rall.at[zz, xx, cc])

    gg[s4] = dot_nn(tsel[s4], grads).astype(BF)
    k_gg, k_inn = alloc(3), alloc(4)
    send(gg.at[s4], gg.at[s4], k_gg, twin)
    send(gg.at[s4], gg.at[s4], k_gg + 1, cross)
    for k in range(1, 4):
        send(inn.at[s4], inn.at[s4], k_inn + k, dev(z, *near(k), t))
    gather.crossed()
    across, corner = gg.at[(1 - xl) * 2 + c], gg.at[(1 - xl) * 2 + 1 - c]
    recv(across, k_gg + 1)
    send(across, across, k_gg + 2, twin)
    for k in range(1, 4):
        xx, cc = near(k)
        recv(inn.at[xx * 2 + cc], k_inn + k)
    int_all[t] = inn[...]
    k_int, k_back, k_int2, k_back2 = alloc(nt), alloc(nt), alloc(nt), alloc(nt)
    for d in range(1, nt):
        send(int_all.at[t], int_all.at[t], k_int + d, dev(z, xl, c, to_t(d)))
    recv(gg.at[xl * 2 + 1 - c], k_gg)
    recv(corner, k_gg + 2)

    bs, br, bo = r["bs"], r["br"], r["bo"]
    depth_all = gg.shape[2]

    def back(d, carry):
        tt = to_t(d)
        block = dot_nt(
            gg[...].reshape(4 * texts, depth_all), wg[pl.ds(pl.multiple_of(tt * chunk, chunk), chunk), :]
        )
        bs[d] = block.astype(BF)
        rcopy(bs.at[d], br.at[d], k_back + d, dev(z, xl, c, tt)).start()
        return carry

    lax.fori_loop(1, nt, back, 0)
    for d in range(1, nt):
        pending.append(rcopy(bs.at[d], br.at[d], k_back + d, dev(z, xl, c, to_t(d))))
    for i in range(1, n_right + 1):
        gather.step(i)
        if i == 1:
            bo[...] = dot_nt(
                gg[...].reshape(4 * texts, depth_all), wg[pl.ds(pl.multiple_of(t * chunk, chunk), chunk), :]
            )
            own_x = dot_nn(h_own, r["outer_v"][t])
            for d in range(1, nt):
                recv(own_r.at[d], k_own + d)
                own_x = own_x + own_r[d].astype(F32)
            own_x = own_x.astype(BF).astype(F32)
    gather.finish()

    routed = dot_nn(wanted[...], rall[...].reshape(total, rall.shape[4]))
    inv_row = routed[:, depth_all : depth_all + 1] + routed[:, depth_all + 1 : depth_all + 2]
    inv_row = inv_row + routed[:, depth_all + 2 : depth_all + 3]
    inn_row = routed[:, depth_all + 3 : depth_all + 4] + routed[:, depth_all + 4 : depth_all + 5]
    inn_row = inn_row + routed[:, depth_all + 5 : depth_all + 6]
    routed = routed[:, :depth_all].astype(BF)
    int_own = r["int_own"]
    int_own[t] = row_tile(inn_row)
    bs2, br2 = r["bs2"], r["br2"]
    for d in range(1, nt):
        bs2[d] = dot_nt(routed, wg[pl.ds(pl.multiple_of(to_t(d) * chunk, chunk), chunk), :]).astype(BF)
        send(bs2.at[d], br2.at[d], k_back2 + d, dev(z, xl, c, to_t(d)))
        send(int_own.at[t], int_own.at[t], k_int2 + d, dev(z, xl, c, to_t(d)))
    own_back = dot_nt(routed, wg[pl.ds(pl.multiple_of(t * chunk, chunk), chunk), :])

    for d in range(1, nt):
        recv(int_all.at[from_t(d)], k_int + d)
    for d in range(1, nt):
        recv(br.at[d], k_back + d)
        bo[...] += br[d].astype(F32)
    gt_s, gt_r = r["gt_s"], r["gt_r"]
    for o in range(4):
        tile = int_all[0, o]
        for d in range(1, nt):
            tile = tile + int_all[d, o]
        marks = tsel[o].astype(F32)
        inv_o = jnp.sum(marks * inv[o].T[:1], axis=1, keepdims=True)
        inn_o = jnp.sum(marks * tile[:1], axis=1, keepdims=True)
        x = dot_nn(tsel[o], xf[o * 128 : (o + 1) * 128, pl.ds(pl.multiple_of(t * chunk, chunk), chunk)])
        grad = inv_o * bo[o * texts : (o + 1) * texts, :] - x * (inv_o * inv_o * inn_o / width)
        gt_s[o] = dot_tn(tsel[o], grad.astype(BF)).astype(BF).reshape(2, 64, chunk)
    k_gt, k_gr = alloc(4), alloc(4)
    for k in range(1, 4):
        xx, cc = near(k)
        send(gt_s.at[pl.ds(2 * xx, 2), cc], gt_r.at[s4], k_gt + k, dev(z, xx, cc, t))
    gt_r[s4] = gt_s[pl.ds(2 * xl, 2), c]

    for d in range(1, nt):
        recv(int_own.at[from_t(d)], k_int2 + d)
        recv(br2.at[d], k_back2 + d)
        own_back = own_back + br2[d].astype(F32)
    tile = int_own[0]
    for d in range(1, nt):
        tile = tile + int_own[d]
    grad = inv_row * own_back - own_x * (inv_row * inv_row * column_of(tile)[:, :1] / width)
    gr_s, gr_r = r["gr_s"], r["gr_r"]
    gr_s[...] = grad.astype(BF).reshape(4, rows, chunk)
    for k in range(1, 4):
        xx, cc = near(k)
        send(gr_s.at[xx * 2 + cc], gr_r.at[s4], k_gr + k, dev(z, xx, cc, t))
    gr_r[s4] = gr_s[s4]
    for k in range(1, 4):
        xx, cc = near(k)
        recv(gt_r.at[xx * 2 + cc], k_gt + k)
    for o in range(4):
        r["gtext"][:, :, o * chunk : (o + 1) * chunk] = gt_r[o]
    for k in range(1, 4):
        xx, cc = near(k)
        recv(gr_r.at[xx * 2 + cc], k_gr + k)
    for o in range(4):
        r["gimage"][:, o * chunk : (o + 1) * chunk] = gr_r[o]
    recv(att_r, k_att)
    r["attended"][c] = att_o[c]
    r["attended"][1 - c] = att_r[...]
    for copy in pending:
        copy.wait_send()


def per_device(
    patches,
    merge_gain,
    merge_bias,
    merge_inner,
    merge_outer,
    slot_target,
    text_embed,
    norm_gain,
    query_weight,
    key_weight,
    value_weight,
    attn_cotangent,
):
    nsec, nt = lax.axis_size("sec"), lax.axis_size("tp")
    nz, ny = nsec // 4, max(nt // 2, 1)
    rows, pw = patches.shape
    hid = merge_inner.shape[1]
    micro, tok, feat = text_embed.shape
    chunk = feat // 4
    seq = tok * nsec
    images = 4 * rows
    total = nz * images
    depth = query_weight.shape[0]
    heads = query_weight.shape[1] // HEAD_DIM
    cols = (heads + 2) * HEAD_DIM
    plane = 512

    vmem, anyspace = pl.BlockSpec(memory_space=pltpu.VMEM), pl.BlockSpec(memory_space=pl.ANY)
    n_right, n_left = nz // 2, max((nz - 1) // 2, 1)
    n_sem = 320
    ins = ["patches", "gain", "bias", "inner", "outer", "slot", "ngain", "text", "wq", "wk", "wv", "cot"]
    outs = ["attended", "gtext", "gimage"]
    scratch = dict(
        pall=((nt, rows, pw), BF),
        inner_v=(merge_inner.shape, BF),
        outer_v=((nt, hid, chunk), BF),
        a=((nt, 4, 2, tok, chunk), BF),
        wg=((nz * depth, cols), BF),
        d_out=((2, tok, heads * HEAD_DIM), BF),
        w_v=((depth, cols), BF),
        gain_v=((depth * nsec // 128, 128), F32),
        kcol=((total, 128), F32),
        wanted=((images, total), BF),
        tsel=((4, 128 - rows, 128), BF),
        isel=((rows, 128), BF),
        own_s=((nt, images, chunk), BF),
        own_r=((nt, images, chunk), BF),
        int_own=((nt, 8, 128), F32),
        bs2=((nt, images, chunk), BF),
        br2=((nt, images, chunk), BF),
        gr_s=((4, rows, chunk), BF),
        gr_r=((4, rows, chunk), BF),
        hall=((nz, 2, 2, rows, hid), BF),
        pick=((images, total), BF),
        place=((plane, images), BF),
        mask=((plane, chunk), F32),
        part_s=((nt, images, chunk), BF),
        part_r=((nt, images, chunk), BF),
        img=((nt, images, chunk), BF),
        xf=((plane, nt * chunk), BF),
        ss=((plane, 128), F32),
        ss_all=((4, 4, 8, 128), F32),
        inv=((4, 128, 128), F32),
        c_s=((3, 128, cols), BF),
        c_r=((3, 128, cols), BF),
        cn=((128, cols), F32),
        qs=((heads, 128, 128), BF),
        kv=((nz, 2, 128, 256), BF),
        dos=((heads, 128, 128), BF),
        ph=((heads, 128, seq), BF),
        ds=((heads, 128, seq), BF),
        att=((heads, 128, 128), BF),
        dq=((heads, 128, 128), BF),
        att_o=((2, tok, heads * HEAD_DIM), BF),
        att_r=((tok, heads * HEAD_DIM), BF),
        dkv=((nz, 256, 256), F32),
        sr=((2, n_right, 128, 256), BF),
        rr=((2, n_right, 128, 256), BF),
        sl=((2, n_left, 128, 256), BF),
        rl=((2, n_left, 128, 256), BF),
        dx_s=((128, 256), BF),
        dx_r=((128, 256), BF),
        gg=((4, 128 - rows, cols), BF),
        inn=((4, 8, 128), F32),
        int_all=((nt, 4, 8, 128), F32),
        bs=((nt, 4 * (128 - rows), chunk), BF),
        br=((nt, 4 * (128 - rows), chunk), BF),
        bo=((4 * (128 - rows), chunk), F32),
        gt_s=((4, 2, tok, chunk), BF),
        gt_r=((4, 2, tok, chunk), BF),
        rall=((nz, 2, 2, rows, cols + 128), BF),
    )
    names = ins + outs + list(scratch) + ["ssem", "rsem", "lsem", "n_sem"]
    call = pl.pallas_call(
        lambda *refs: kernel(nz, nt, ny, names, *refs, n_sem),
        out_shape=(
            jax.ShapeDtypeStruct((micro, tok, heads * HEAD_DIM), BF),
            jax.ShapeDtypeStruct((micro, tok, feat), BF),
            jax.ShapeDtypeStruct((rows, feat), BF),
        ),
        in_specs=[vmem if n in ("gain", "bias", "slot", "ngain") else anyspace for n in ins],
        out_specs=(vmem,) * 3,
        scratch_shapes=[pltpu.VMEM(shape, dtype) for shape, dtype in scratch.values()]
        + [
            pltpu.SemaphoreType.DMA((n_sem,)),
            pltpu.SemaphoreType.DMA((n_sem,)),
            pltpu.SemaphoreType.DMA((24,)),
        ],
        compiler_params=pltpu.CompilerParams(
            collective_id=0, has_side_effects=True, vmem_limit_bytes=56 * 1024 * 1024
        ),
        name="merged_step",
    )
    return call(
        patches,
        merge_gain,
        merge_bias,
        merge_inner,
        merge_outer,
        slot_target,
        norm_gain,
        text_embed,
        query_weight,
        key_weight,
        value_weight,
        attn_cotangent,
    )


def solution(mesh):
    return jax.shard_map(
        per_device,
        mesh=mesh,
        in_specs=(
            P("sec", "tp"),
            P(),
            P(),
            P(None, "tp"),
            P("tp", None),
            P(),
            P(None, "sec", "tp"),
            P(),
            P("sec", "tp"),
            P("sec", "tp"),
            P("sec", "tp"),
            P(None, "sec", "tp"),
        ),
        out_specs=(P(None, "sec", "tp"), P(None, "sec", "tp"), P("sec", "tp")),
        check_vma=False,
    )
```

```python
import functools
import math

import jax
import jax.numpy as jnp
from jax import lax
from jax.experimental import pallas as pl
from jax.experimental.pallas import tpu as pltpu
from jax.sharding import PartitionSpec as P

HEAD_DIM = 128
BF = jnp.bfloat16
F32 = jnp.float32
MESH = pl.DeviceIdType.MESH


def dot_nn(a, b):
    return jnp.dot(a, b, preferred_element_type=F32)


def dot_nt(a, b):
    return lax.dot_general(a, b, (((1,), (1,)), ((), ())), preferred_element_type=F32)


def dot_tn(a, b):
    return lax.dot_general(a, b, (((0,), (0,)), ((), ())), preferred_element_type=F32)


def row_tile(column):
    return jnp.broadcast_to(column, (128, 128)).T[:8]


def column_of(tile):
    return jnp.broadcast_to(tile[0:1, :], (128, 128)).T


def kernel(nz, nt, ny, names, *refs):
    r = dict(zip(names, refs))
    patches, gain, bias, inner, outer = (r[n] for n in ("patches", "gain", "bias", "inner", "outer"))
    text, cot = r["text"], r["cot"]
    ssem, rsem, lsem = r["ssem"], r["rsem"], r["lsem"]
    sec, t = lax.axis_index("sec"), lax.axis_index("tp")
    z, s4 = lax.div(sec, 4), lax.rem(sec, 4)
    xl, c = lax.div(s4, 2), lax.rem(s4, 2)
    nxh = nt // ny
    xh, y = lax.div(t, ny), lax.rem(t, ny)
    rows, pw = patches.shape
    chunk = text.shape[2] // 4
    plane = 4 * 128
    images = 4 * rows
    width = text.shape[2] * nt
    seq = nz * 256
    scale = 1.0 / math.sqrt(HEAD_DIM)

    def zmod(v):
        return lax.rem(v + nz, nz)

    def to_t(d):
        dx, dy = d // ny, d % ny
        return lax.rem(xh + dx, nxh) * ny + lax.rem(y + dy, ny)

    def from_t(d):
        dx, dy = d // ny, d % ny
        return lax.rem(xh + nxh - dx, nxh) * ny + lax.rem(y + ny - dy, ny)

    def near(k):
        a = 1 - xl if k // 2 else xl
        b = 1 - c if k % 2 else c
        return a, b

    def dev(zz, xx, cc, tt):
        return (zz * 4 + xx * 2 + cc, tt)

    counter = [0]
    pending = []

    def alloc(n):
        first = counter[0]
        counter[0] += n
        assert counter[0] <= r["n_sem"]
        return first

    def rcopy(src, dst, k, to):
        return pltpu.make_async_remote_copy(
            src_ref=src, dst_ref=dst, send_sem=ssem.at[k], recv_sem=rsem.at[k], device_id=to, device_id_type=MESH
        )

    right, left = dev(zmod(z + 1), xl, c, t), dev(zmod(z - 1), xl, c, t)
    cross = dev(z, 1 - xl, c, t)
    twin = dev(z, xl, 1 - c, t)

    def send(src, dst, k, to):
        copy = rcopy(src, dst, k, to)
        copy.start()
        pending.append(copy)

    def recv(dst, k):
        rcopy(dst, dst, k, twin).wait_recv()

    locals_ = [0]

    def lcopy(src, dst):
        copy = pltpu.make_async_copy(src, dst, lsem.at[locals_[0]])
        locals_[0] += 1
        copy.start()
        return copy

    n_right, n_left = nz // 2, (nz - 1) // 2

    class Ring:
        def __init__(self, slot):
            self.slot = slot
            self.kr, self.kl = alloc(n_right), alloc(n_left)

        def start(self):
            mine = self.slot(z)
            send(mine, mine, self.kr, right)
            if n_left:
                send(mine, mine, self.kl, left)

        def step(self, i):
            came = []
            ref = self.slot(zmod(z - i))
            recv(ref, self.kr + i - 1)
            came.append(zmod(z - i))
            if i < n_right:
                send(ref, ref, self.kr + i, right)
            if i <= n_left:
                ref = self.slot(zmod(z + i))
                recv(ref, self.kl + i - 1)
                came.append(zmod(z + i))
                if i < n_left:
                    send(ref, ref, self.kl + i, left)
            return came

    pall, a_ref, wg, d_out, w_v = r["pall"], r["a"], r["wg"], r["d_out"], r["w_v"]
    own_copies = [
        lcopy(patches, pall.at[t]),
        lcopy(
            text.at[:, :, pl.ds(pl.multiple_of(s4 * chunk, chunk), chunk)], a_ref.at[t, pl.ds(2 * xl, 2), c]
        ),
        lcopy(cot.at[c], d_out.at[c]),
    ]
    w_copies = []
    first = 0
    for name in ("wq", "wk", "wv"):
        n = r[name].shape[1]
        w_copies.append(lcopy(r[name], w_v.at[:, pl.ds(first, n)]))
        first += n
    inner_copy = lcopy(inner, r["inner_v"])
    outer_copies = [
        lcopy(outer.at[:, pl.ds(pl.multiple_of((tt * 4 + s4) * chunk, chunk), chunk)], r["outer_v"].at[tt])
        for tt in range(nt)
    ]

    barrier = pltpu.get_barrier_semaphore()
    peers = [dev(z, xl, c, to_t(d)) for d in range(1, nt)]
    peers += [dev(z, *near(k), t) for k in range(1, 4)] + [right, left]
    for peer in peers:
        pl.semaphore_signal(barrier, inc=1, device_id=peer, device_id_type=MESH)
    pl.semaphore_wait(barrier, len(peers))

    k_patch = alloc(nt)
    for d in range(1, nt):
        send(patches, pall.at[t], k_patch + d, dev(z, xl, c, to_t(d)))
    k_text = alloc(4)
    for k in range(1, 4):
        xx, cc = near(k)
        part = text.at[:, :, pl.ds(pl.multiple_of((xx * 2 + cc) * chunk, chunk), chunk)]
        send(part, a_ref.at[t, pl.ds(2 * xl, 2), c], k_text + k, dev(z, xx, cc, t))
    k_cot = alloc(1)
    send(cot.at[1 - c], d_out.at[c], k_cot, twin)

    r["gain_v"][...] = r["ngain"][...].reshape(r["gain_v"].shape)
    for copy in w_copies:
        copy.wait()
    for i in range(2):
        factor = column_of(r["gain_v"][pl.ds(sec * 2 + i, 1), :])[:, :1]
        rows_i = pl.ds(pl.multiple_of(z * 256 + i * 128, 128), 128)
        wg[rows_i, :] = (w_v[i * 128 : (i + 1) * 128, :].astype(F32) * factor).astype(BF)
    ring_w = Ring(lambda zz: wg.at[pl.ds(pl.multiple_of(zz * 256, 256), 256)])
    ring_w.start()

    pick, place, mask, kcol = r["pick"], r["place"], r["mask"], r["kcol"]
    total = nz * images
    slot = r["slot"][...].reshape(1, total)
    bits = seq.bit_length() - 1
    batch, pos = slot >> bits, slot & (seq - 1)
    key = ((pos >> 8) * plane + ((pos >> 7) & 1) * 256 + batch * 128 + (pos & 127)).astype(F32)
    for i in range(total // 128):
        kcol[i * 128 : (i + 1) * 128, :] = column_of(key[:, i * 128 : (i + 1) * 128])
    rank = jnp.sum(jnp.where(kcol[...][:, :1] < key, 1.0, 0.0), axis=0, keepdims=True)
    wide_rows = lax.broadcasted_iota(jnp.int32, (images, total), 0) + z * images
    pick[...] = jnp.where(rank == wide_rows.astype(F32), 1.0, 0.0).astype(BF)
    wide_rows = lax.broadcasted_iota(jnp.int32, (plane, total), 0) + z * plane
    stands = jnp.where(key == wide_rows.astype(F32), 1.0, 0.0).astype(BF)
    place[...] = dot_nt(stands, pick[...]).astype(BF)
    mask[...] = dot_nn(place[...], jnp.ones((images, chunk), BF))
    own_key = kcol[pl.ds(pl.multiple_of(z * images, images), images), :][:, :1]
    own_rank = jnp.sum(jnp.where(key < own_key, 1.0, 0.0), axis=1, keepdims=True)
    wanted, tsel, isel = r["wanted"], r["tsel"], r["isel"]
    wanted[...] = jnp.where(
        own_rank == lax.broadcasted_iota(jnp.int32, (images, total), 1).astype(F32), 1.0, 0.0
    ).astype(BF)
    earlier = jnp.where(
        lax.broadcasted_iota(jnp.int32, (128, 128), 0) < lax.broadcasted_iota(jnp.int32, (128, 128), 1), 1.0, 0.0
    ).astype(BF)

    def select(flags, count):
        nth = dot_nn(flags[:8].astype(BF), earlier)[:1]
        return jnp.where(
            nth == lax.broadcasted_iota(jnp.int32, (count, 128), 0).astype(F32), flags[:1], 0.0
        ).astype(BF)

    texts = 128 - rows
    for o in range(4):
        tsel[o] = select(1.0 - mask[o * 128 : (o + 1) * 128, :128].T, texts)
    isel[...] = select(mask[pl.ds(pl.multiple_of(s4 * 128, 128), 128), :128].T, rows)

    for copy in own_copies:
        copy.wait()

    for k in range(1, 4):
        xx, cc = near(k)
        recv(a_ref.at[t, pl.ds(2 * xx, 2), cc], k_text + k)
    k_a = alloc(nt)

    across_x = range(ny, nt, ny)
    for d in [*range(1, ny), *across_x]:
        send(a_ref.at[t], a_ref.at[t], k_a + d, dev(z, xl, c, to_t(d)))

    def text_on():
        for first in across_x:
            ref = a_ref.at[from_t(first)]
            recv(ref, k_a + first)
            for d in range(1, ny):
                send(ref, ref, k_a + first + d, dev(z, xl, c, to_t(d)))

    for d in range(1, nt):
        recv(pall.at[from_t(d)], k_patch + d)
    inner_copy.wait()
    vit = gain.shape[0]
    per = vit // pw
    hidden = None
    for piece in range(nt // per):
        wide = jnp.concatenate([pall[piece * per + i] for i in range(per)], axis=1).astype(F32)
        centre = jnp.mean(wide, axis=1, keepdims=True)
        shifted = wide - centre
        spread = jnp.mean(shifted * shifted, axis=1, keepdims=True)
        normed = (shifted * lax.rsqrt(spread + 1e-06) * gain[...].reshape(1, vit) + bias[...].reshape(1, vit)).astype(BF)
        term = dot_nn(normed, r["inner_v"][piece * vit : (piece + 1) * vit, :])
        hidden = term if hidden is None else hidden + term
    hidden = (0.5 * hidden * (1.0 + lax.erf(hidden * math.sqrt(0.5)))).astype(BF)

    class Gather:
        def __init__(self, slot_of):
            self.slot_of = slot_of
            self.k_cross, self.k_twin = alloc(1), alloc(2 * nz)
            mine = slot_of(z, xl, c)
            send(mine, mine, self.k_cross, cross)
            self.rings = [Ring(lambda zz: slot_of(zz, xl, c)), Ring(lambda zz: slot_of(zz, 1 - xl, c))]
            self.done = []
            self.rings[0].start()
            self.arrived(z, xl)

        def arrived(self, zz, xx):
            ref = self.slot_of(zz, xx, c)
            send(ref, ref, self.k_twin + len(self.done), twin)
            self.done.append((zz, xx))

        def crossed(self):
            recv(self.slot_of(z, 1 - xl, c), self.k_cross)
            self.rings[1].start()
            self.arrived(z, 1 - xl)

        def step(self, i):
            for ring, xx in zip(self.rings, (xl, 1 - xl)):
                for zz in ring.step(i):
                    self.arrived(zz, xx)

        def finish(self):
            for j, (zz, xx) in enumerate(self.done):
                recv(self.slot_of(zz, xx, 1 - c), self.k_twin + j)

    hall = r["hall"]
    hall[z, xl, c] = hidden
    ring_w.step(1)
    gather = Gather(lambda zz, xx, cc: hall.at[zz, xx, cc])
    gather.crossed()
    text_on()
    for i in range(1, n_right + 1):
        gather.step(i)
    gather.finish()
    if n_right > 2:
        ring_w.step(2)

    hp = dot_nn(pick[...], hall[...].reshape(total, hall.shape[4])).astype(BF)
    for copy in outer_copies:
        copy.wait()
    part_s, part_r, img = r["part_s"], r["part_r"], r["img"]
    k_part, k_img = alloc(nt), alloc(nt)
    for d in range(1, nt):
        part_s[d] = dot_nn(hp, r["outer_v"][to_t(d)]).astype(BF)
        send(part_s.at[d], part_r.at[d], k_part + d, dev(z, xl, c, to_t(d)))
    mine = dot_nn(hp, r["outer_v"][t])
    for d in range(1, nt):
        recv(part_r.at[d], k_part + d)
        mine = mine + part_r[d].astype(F32)
    img[t] = mine.astype(BF)
    for d in range(1, nt):
        send(img.at[t], img.at[t], k_img + d, dev(z, xl, c, to_t(d)))
    if n_right > 3:
        ring_w.step(3)

    xf, ss = r["xf"], r["ss"]

    def take(tt):
        placed = dot_nn(place[...], img[tt])
        x = jnp.where(mask[...] > 0.5, placed, a_ref[tt].reshape(plane, chunk).astype(F32))
        xf[:, pl.ds(pl.multiple_of(tt * chunk, chunk), chunk)] = x.astype(BF)
        x = x * x
        return x[:, :128] + x[:, 128:]

    ss[...] = take(t)

    def take_next(d, carry):
        @pl.when(lax.rem(d, ny) != 0)
        def _():
            recv(a_ref.at[from_t(d)], k_a + d)

        recv(img.at[from_t(d)], k_img + d)
        ss[...] += take(from_t(d))
        return carry

    lax.fori_loop(1, nt, take_next, 0)
    ss_all, inv = r["ss_all"], r["inv"]
    squares = jnp.sum(ss[...], axis=1, keepdims=True)
    for o in range(4):
        ss_all[s4, o] = row_tile(squares[o * 128 : (o + 1) * 128])
    k_ss, k_c = alloc(4), alloc(4)
    for k in range(1, 4):
        send(ss_all.at[s4], ss_all.at[s4], k_ss + k, dev(z, *near(k), t))
    ring_w.step(n_right)

    c_s, c_r, cn = r["c_s"], r["c_r"], r["cn"]
    def project(xx, cc):
        return dot_nn(xf[pl.ds(pl.multiple_of((xx * 2 + cc) * 128, 128), 128), :], wg[...])

    c_s[0] = project(1 - xl, 1 - c).astype(BF)
    send(c_s.at[0], c_r.at[0], k_c, twin)
    c_s[1] = project(xl, 1 - c).astype(BF)
    send(c_s.at[1], c_r.at[1], k_c + 1, twin)
    other = project(1 - xl, c)
    recv(c_r.at[0], k_c)
    c_s[2] = (other + c_r[0].astype(F32)).astype(BF)
    send(c_s.at[2], c_r.at[2], k_c + 2, cross)
    cn[...] = project(xl, c)
    for k in range(1, 4):
        xx, cc = near(k)
        recv(ss_all.at[xx * 2 + cc], k_ss + k)
    for o in range(4):
        tile = ss_all[0, o] + ss_all[1, o] + ss_all[2, o] + ss_all[3, o]
        inv[o] = column_of(lax.rsqrt(tile / width + 1e-06))
    projected = cn[...]
    for k in range(1, 3):
        recv(c_r.at[k], k_c + k)
        projected = projected + c_r[k].astype(F32)
    projected = projected * inv[s4][:, :1]
    cn[...] = projected
    heads = (projected.shape[1] - 2 * HEAD_DIM) // HEAD_DIM
    qs, kv, dos = r["qs"], r["kv"], r["dos"]
    for h in range(heads):
        qs[h] = projected[:, h * 128 : (h + 1) * 128].astype(BF)
    kv[z, xl] = projected[:, heads * 128 :].astype(BF)

    k_kv = alloc(1)
    send(kv.at[z, xl], kv.at[z, xl], k_kv, cross)
    rings = [Ring(lambda zz: kv.at[zz, xl]), Ring(lambda zz: kv.at[zz, 1 - xl])]
    rings[0].start()
    recv(kv.at[z, 1 - xl], k_kv)
    rings[1].start()
    own_s, own_r = r["own_s"], r["own_r"]
    k_own = alloc(nt)
    h_own = hall[z].reshape(images, hall.shape[4])
    for d in range(1, nt):
        own_s[d] = dot_nn(h_own, r["outer_v"][to_t(d)]).astype(BF)
        send(own_s.at[d], own_r.at[d], k_own + d, dev(z, xl, c, to_t(d)))
    recv(d_out.at[1 - c], k_cot)
    for h in range(heads):
        dos[h] = d_out[:, :, h * 128 : (h + 1) * 128].reshape(128, 128)
    for i in range(1, n_right + 1):
        rings[0].step(i)
        rings[1].step(i)

    ph, ds, att, dq = r["ph"], r["ds"], r["att"], r["dq"]

    def head(h, carry):
        keys = kv[:, :, :, :128].reshape(seq, 128)
        values = kv[:, :, :, 128:].reshape(seq, 128)
        scores = dot_nt(qs[h], keys) * scale
        query_pos = z * 256 + xl * 128 + lax.broadcasted_iota(jnp.int32, (128, seq), 0)
        scores = jnp.where(lax.broadcasted_iota(jnp.int32, (128, seq), 1) <= query_pos, scores, -1e30)
        raw = jnp.exp(scores - jnp.max(scores, axis=1, keepdims=True))
        probs = raw / jnp.sum(raw, axis=1, keepdims=True)
        half = probs.astype(BF)
        ph[h] = half
        att[h] = dot_nn(half, values).astype(BF)
        grad_probs = dot_nt(dos[h], values)
        delta = jnp.sum(probs * grad_probs, axis=1, keepdims=True)
        grad = (probs * (grad_probs - delta)).astype(BF)
        ds[h] = grad
        dq[h] = (dot_nn(grad, keys) * scale).astype(BF)
        return carry

    lax.fori_loop(0, heads, head, 0)
    att_o, att_r = r["att_o"], r["att_r"]
    for h in range(heads):
        att_o[:, :, h * 128 : (h + 1) * 128] = att[h].reshape(2, 64, 128)
    k_att = alloc(1)
    send(att_o.at[1 - c], att_r, k_att, twin)

    sr, rr, sl, rl = r["sr"], r["rr"], r["sl"], r["rl"]
    kr, kl = alloc(2 * n_right), alloc(2 * max(n_left, 1))
    dx_s, dx_r = r["dx_s"], r["dx_r"]
    k_dx = alloc(1)

    def make(n, carry):
        zz, xx = lax.rem(z + n_right + lax.div(n, 2), nz), lax.rem(n, 2)
        lanes = pl.ds(pl.multiple_of((zz * 2 + xx) * 128, 128), 128)
        grad_keys = dot_tn(ds[:, :, lanes].reshape(heads * 128, 128), qs[...].reshape(heads * 128, 128))
        grad_values = dot_tn(ph[:, :, lanes].reshape(heads * 128, 128), dos[...].reshape(heads * 128, 128))
        dkv[zz, xx, :, :128] = grad_keys
        dkv[zz, xx, :, 128:] = grad_values
        return carry

    dkv = r["dkv"]
    lax.fori_loop(0, 4, make, 0)
    halves = ((0, 1 - xl), (1, xl))
    for i in range(n_right + 1):
        if i == 1:
            lax.fori_loop(4, 2 * nz, make, 0)
        for half, xx in halves:
            value = dkv[zmod(z + n_right - i), xx]
            if i:
                recv(rr.at[half, i - 1], kr + 2 * (i - 1) + half)
                value = value + rr[half, i - 1].astype(F32)
            if i < n_right:
                sr[half, i] = value.astype(BF)
                send(sr.at[half, i], rr.at[half, i], kr + 2 * i + half, right)
            elif half == 0:
                if n_left:
                    value = value + rl[half, n_left - 1].astype(F32)
                dx_s[...] = value.astype(BF)
                send(dx_s, dx_r, k_dx, cross)
            else:
                if n_left:
                    value = value + rl[half, n_left - 1].astype(F32)
                grad_kv = value
        for half, xx in halves:
            if n_left and i <= n_left:
                if i:
                    recv(rl.at[half, i - 1], kl + 2 * (i - 1) + half)
                if i < n_left:
                    value = dkv[zmod(z - n_left + i), xx]
                    if i:
                        value = value + rl[half, i - 1].astype(F32)
                    sl[half, i] = value.astype(BF)
                    send(sl.at[half, i], rl.at[half, i], kl + 2 * i + half, left)
    recv(dx_r, k_dx)
    grad_kv = grad_kv + dx_r[...].astype(F32)

    gg, inn, int_all = r["gg"], r["inn"], r["int_all"]
    pieces = [dq[h] for h in range(heads)]
    pieces += [(grad_kv[:, :128] * scale).astype(BF), grad_kv[:, 128:].astype(BF)]
    grads = jnp.concatenate(pieces, axis=1)
    inn_tile = row_tile(jnp.sum(grads.astype(F32) * cn[...], axis=1, keepdims=True))
    inn[s4] = inn_tile
    marks = isel[...].astype(F32)
    beside = (
        jnp.sum(marks * inv[s4].T[:1], axis=1, keepdims=True),
        jnp.sum(marks * inn_tile[:1], axis=1, keepdims=True),
    )
    lane = lax.broadcasted_iota(jnp.int32, (rows, 128), 1)
    extra = jnp.zeros((rows, 128), F32)
    for n, value in enumerate(beside):
        for m in range(3):
            part = value.astype(BF).astype(F32)
            extra = jnp.where(lane == 3 * n + m, part, extra)
            value = value - part
    rall = r["rall"]
    rall[z, xl, c] = jnp.concatenate([dot_nn(isel[...], grads).astype(BF), extra.astype(BF)], axis=1)
    gather = Gather(lambda zz, xx, cc: rall.at[zz, xx, cc])

    gg[s4] = dot_nn(tsel[s4], grads).astype(BF)
    k_gg, k_inn = alloc(3), alloc(4)
    send(gg.at[s4], gg.at[s4], k_gg, twin)
    send(gg.at[s4], gg.at[s4], k_gg + 1, cross)
    for k in range(1, 4):
        send(inn.at[s4], inn.at[s4], k_inn + k, dev(z, *near(k), t))
    k_int, k_back, k_int2, k_back2 = alloc(nt), alloc(2 * nt), alloc(nt), alloc(nt)

    bs, br, bo = r["bs"], r["br"], r["bo"]
    depth_all = gg.shape[2]

    def back(half, xx):
        def one(tt):
            lines = gg[pl.ds(2 * xx, 2)].reshape(2 * texts, depth_all)
            return dot_nt(lines, wg[pl.ds(pl.multiple_of(tt * chunk, chunk), chunk), :])

        def step(d, carry):
            tt = to_t(d)
            bs[d, xx] = one(tt).astype(BF)
            rcopy(bs.at[d, xx], br.at[d, xx], k_back + 2 * d + half, dev(z, xl, c, tt)).start()
            return carry

        lax.fori_loop(1, nt, step, 0)
        for d in range(1, nt):
            pending.append(rcopy(bs.at[d, xx], br.at[d, xx], k_back + 2 * d + half, dev(z, xl, c, to_t(d))))
        return one

    recv(gg.at[xl * 2 + 1 - c], k_gg)
    near_half = back(0, xl)
    gather.crossed()
    across, corner = gg.at[(1 - xl) * 2 + c], gg.at[(1 - xl) * 2 + 1 - c]
    recv(across, k_gg + 1)
    send(across, across, k_gg + 2, twin)
    for k in range(1, 4):
        xx, cc = near(k)
        recv(inn.at[xx * 2 + cc], k_inn + k)
    int_all[t] = inn[...]
    for d in range(1, nt):
        send(int_all.at[t], int_all.at[t], k_int + d, dev(z, xl, c, to_t(d)))
    recv(corner, k_gg + 2)
    far_half = back(1, 1 - xl)
    for i in range(1, n_right + 1):
        gather.step(i)
        if i == 1:
            bo[xl] = near_half(t)
            bo[1 - xl] = far_half(t)
            own_x = dot_nn(h_own, r["outer_v"][t])
            for d in range(1, nt):
                recv(own_r.at[d], k_own + d)
                own_x = own_x + own_r[d].astype(F32)
            own_x = own_x.astype(BF).astype(F32)
    gather.finish()

    routed = dot_nn(wanted[...], rall[...].reshape(total, rall.shape[4]))
    inv_row = routed[:, depth_all : depth_all + 1] + routed[:, depth_all + 1 : depth_all + 2]
    inv_row = inv_row + routed[:, depth_all + 2 : depth_all + 3]
    inn_row = routed[:, depth_all + 3 : depth_all + 4] + routed[:, depth_all + 4 : depth_all + 5]
    inn_row = inn_row + routed[:, depth_all + 5 : depth_all + 6]
    routed = routed[:, :depth_all].astype(BF)
    int_own = r["int_own"]
    int_own[t] = row_tile(inn_row)
    bs2, br2 = r["bs2"], r["br2"]
    for d in range(1, nt):
        bs2[d] = dot_nt(routed, wg[pl.ds(pl.multiple_of(to_t(d) * chunk, chunk), chunk), :]).astype(BF)
        send(bs2.at[d], br2.at[d], k_back2 + d, dev(z, xl, c, to_t(d)))
        send(int_own.at[t], int_own.at[t], k_int2 + d, dev(z, xl, c, to_t(d)))
    own_back = dot_nt(routed, wg[pl.ds(pl.multiple_of(t * chunk, chunk), chunk), :])

    for d in range(1, nt):
        recv(int_all.at[from_t(d)], k_int + d)
    for d in range(1, nt):
        for half, xx in ((0, xl), (1, 1 - xl)):
            recv(br.at[d, xx], k_back + 2 * d + half)
        bo[...] += br[d].astype(F32)
    gt_s, gt_r = r["gt_s"], r["gt_r"]
    for o in range(4):
        tile = int_all[0, o]
        for d in range(1, nt):
            tile = tile + int_all[d, o]
        marks = tsel[o].astype(F32)
        inv_o = jnp.sum(marks * inv[o].T[:1], axis=1, keepdims=True)
        inn_o = jnp.sum(marks * tile[:1], axis=1, keepdims=True)
        x = dot_nn(tsel[o], xf[o * 128 : (o + 1) * 128, pl.ds(pl.multiple_of(t * chunk, chunk), chunk)])
        grad = inv_o * bo[o // 2, o % 2 * texts : (o % 2 + 1) * texts, :] - x * (inv_o * inv_o * inn_o / width)
        gt_s[o] = dot_tn(tsel[o], grad.astype(BF)).astype(BF).reshape(2, 64, chunk)
    k_gt, k_gr = alloc(4), alloc(4)
    for k in range(1, 4):
        xx, cc = near(k)
        send(gt_s.at[pl.ds(2 * xx, 2), cc], gt_r.at[s4], k_gt + k, dev(z, xx, cc, t))
    gt_r[s4] = gt_s[pl.ds(2 * xl, 2), c]

    for d in range(1, nt):
        recv(int_own.at[from_t(d)], k_int2 + d)
        recv(br2.at[d], k_back2 + d)
        own_back = own_back + br2[d].astype(F32)
    tile = int_own[0]
    for d in range(1, nt):
        tile = tile + int_own[d]
    grad = inv_row * own_back - own_x * (inv_row * inv_row * column_of(tile)[:, :1] / width)
    gr_s, gr_r = r["gr_s"], r["gr_r"]
    gr_s[...] = grad.astype(BF).reshape(4, rows, chunk)
    for k in range(1, 4):
        xx, cc = near(k)
        send(gr_s.at[xx * 2 + cc], gr_r.at[s4], k_gr + k, dev(z, xx, cc, t))
    gr_r[s4] = gr_s[s4]
    for k in range(1, 4):
        xx, cc = near(k)
        recv(gt_r.at[xx * 2 + cc], k_gt + k)
    for o in range(4):
        r["gtext"][:, :, o * chunk : (o + 1) * chunk] = gt_r[o]
    for k in range(1, 4):
        xx, cc = near(k)
        recv(gr_r.at[xx * 2 + cc], k_gr + k)
    for o in range(4):
        r["gimage"][:, o * chunk : (o + 1) * chunk] = gr_r[o]
    recv(att_r, k_att)
    r["attended"][c] = att_o[c]
    r["attended"][1 - c] = att_r[...]
    for copy in pending:
        copy.wait_send()


def per_device(
    patches,
    merge_gain,
    merge_bias,
    merge_inner,
    merge_outer,
    slot_target,
    text_embed,
    norm_gain,
    query_weight,
    key_weight,
    value_weight,
    attn_cotangent,
):
    nsec, nt = lax.axis_size("sec"), lax.axis_size("tp")
    nz, ny = nsec // 4, max(nt // 2, 1)
    rows, pw = patches.shape
    hid = merge_inner.shape[1]
    micro, tok, feat = text_embed.shape
    chunk = feat // 4
    seq = tok * nsec
    images = 4 * rows
    total = nz * images
    depth = query_weight.shape[0]
    heads = query_weight.shape[1] // HEAD_DIM
    cols = (heads + 2) * HEAD_DIM
    plane = 512

    vmem, anyspace = pl.BlockSpec(memory_space=pltpu.VMEM), pl.BlockSpec(memory_space=pl.ANY)
    n_right, n_left = nz // 2, max((nz - 1) // 2, 1)
    n_sem = 320
    ins = ["patches", "gain", "bias", "inner", "outer", "slot", "ngain", "text", "wq", "wk", "wv", "cot"]
    outs = ["attended", "gtext", "gimage"]
    scratch = dict(
        pall=((nt, rows, pw), BF),
        inner_v=(merge_inner.shape, BF),
        outer_v=((nt, hid, chunk), BF),
        a=((nt, 4, 2, tok, chunk), BF),
        wg=((nz * depth, cols), BF),
        d_out=((2, tok, heads * HEAD_DIM), BF),
        w_v=((depth, cols), BF),
        gain_v=((depth * nsec // 128, 128), F32),
        kcol=((total, 128), F32),
        wanted=((images, total), BF),
        tsel=((4, 128 - rows, 128), BF),
        isel=((rows, 128), BF),
        own_s=((nt, images, chunk), BF),
        own_r=((nt, images, chunk), BF),
        int_own=((nt, 8, 128), F32),
        bs2=((nt, images, chunk), BF),
        br2=((nt, images, chunk), BF),
        gr_s=((4, rows, chunk), BF),
        gr_r=((4, rows, chunk), BF),
        hall=((nz, 2, 2, rows, hid), BF),
        pick=((images, total), BF),
        place=((plane, images), BF),
        mask=((plane, chunk), F32),
        part_s=((nt, images, chunk), BF),
        part_r=((nt, images, chunk), BF),
        img=((nt, images, chunk), BF),
        xf=((plane, nt * chunk), BF),
        ss=((plane, 128), F32),
        ss_all=((4, 4, 8, 128), F32),
        inv=((4, 128, 128), F32),
        c_s=((3, 128, cols), BF),
        c_r=((3, 128, cols), BF),
        cn=((128, cols), F32),
        qs=((heads, 128, 128), BF),
        kv=((nz, 2, 128, 256), BF),
        dos=((heads, 128, 128), BF),
        ph=((heads, 128, seq), BF),
        ds=((heads, 128, seq), BF),
        att=((heads, 128, 128), BF),
        dq=((heads, 128, 128), BF),
        att_o=((2, tok, heads * HEAD_DIM), BF),
        att_r=((tok, heads * HEAD_DIM), BF),
        sr=((2, n_right, 128, 256), BF),
        rr=((2, n_right, 128, 256), BF),
        sl=((2, n_left, 128, 256), BF),
        rl=((2, n_left, 128, 256), BF),
        dkv=((nz, 2, 128, 256), F32),
        dx_s=((128, 256), BF),
        dx_r=((128, 256), BF),
        gg=((4, 128 - rows, cols), BF),
        inn=((4, 8, 128), F32),
        int_all=((nt, 4, 8, 128), F32),
        bs=((nt, 2, 2 * (128 - rows), chunk), BF),
        br=((nt, 2, 2 * (128 - rows), chunk), BF),
        bo=((2, 2 * (128 - rows), chunk), F32),
        gt_s=((4, 2, tok, chunk), BF),
        gt_r=((4, 2, tok, chunk), BF),
        rall=((nz, 2, 2, rows, cols + 128), BF),
    )
    names = ins + outs + list(scratch) + ["ssem", "rsem", "lsem", "n_sem"]
    call = pl.pallas_call(
        lambda *refs: kernel(nz, nt, ny, names, *refs, n_sem),
        out_shape=(
            jax.ShapeDtypeStruct((micro, tok, heads * HEAD_DIM), BF),
            jax.ShapeDtypeStruct((micro, tok, feat), BF),
            jax.ShapeDtypeStruct((rows, feat), BF),
        ),
        in_specs=[vmem if n in ("gain", "bias", "slot", "ngain") else anyspace for n in ins],
        out_specs=(vmem,) * 3,
        scratch_shapes=[pltpu.VMEM(shape, dtype) for shape, dtype in scratch.values()]
        + [
            pltpu.SemaphoreType.DMA((n_sem,)),
            pltpu.SemaphoreType.DMA((n_sem,)),
            pltpu.SemaphoreType.DMA((24,)),
        ],
        compiler_params=pltpu.CompilerParams(
            collective_id=0, has_side_effects=True, vmem_limit_bytes=56 * 1024 * 1024
        ),
        name="merged_step",
    )
    return call(
        patches,
        merge_gain,
        merge_bias,
        merge_inner,
        merge_outer,
        slot_target,
        norm_gain,
        text_embed,
        query_weight,
        key_weight,
        value_weight,
        attn_cotangent,
    )


def solution(mesh):
    return jax.shard_map(
        per_device,
        mesh=mesh,
        in_specs=(
            P("sec", "tp"),
            P(),
            P(),
            P(None, "tp"),
            P("tp", None),
            P(),
            P(None, "sec", "tp"),
            P(),
            P("sec", "tp"),
            P("sec", "tp"),
            P("sec", "tp"),
            P(None, "sec", "tp"),
        ),
        out_specs=(P(None, "sec", "tp"), P(None, "sec", "tp"), P("sec", "tp")),
        check_vma=False,
    )
```

```python
import functools
import math

import jax
import jax.numpy as jnp
from jax import lax
from jax.experimental import pallas as pl
from jax.experimental.pallas import tpu as pltpu
from jax.sharding import PartitionSpec as P

HEAD_DIM = 128
BF = jnp.bfloat16
F32 = jnp.float32
MESH = pl.DeviceIdType.MESH


def dot_nn(a, b):
    return jnp.dot(a, b, preferred_element_type=F32)


def dot_nt(a, b):
    return lax.dot_general(a, b, (((1,), (1,)), ((), ())), preferred_element_type=F32)


def dot_tn(a, b):
    return lax.dot_general(a, b, (((0,), (0,)), ((), ())), preferred_element_type=F32)


def row_tile(column):
    return jnp.broadcast_to(column, (128, 128)).T[:8]


def column_of(tile):
    return jnp.broadcast_to(tile[0:1, :], (128, 128)).T


def kernel(nz, nt, ny, names, *refs):
    r = dict(zip(names, refs))
    patches, gain, bias, inner, outer = (r[n] for n in ("patches", "gain", "bias", "inner", "outer"))
    text, cot = r["text"], r["cot"]
    ssem, rsem, lsem = r["ssem"], r["rsem"], r["lsem"]
    sec, t = lax.axis_index("sec"), lax.axis_index("tp")
    z, s4 = lax.div(sec, 4), lax.rem(sec, 4)
    xl, c = lax.div(s4, 2), lax.rem(s4, 2)
    nxh = nt // ny
    xh, y = lax.div(t, ny), lax.rem(t, ny)
    rows, pw = patches.shape
    chunk = text.shape[2] // 4
    plane = 4 * 128
    images = 4 * rows
    width = text.shape[2] * nt
    seq = nz * 256
    scale = 1.0 / math.sqrt(HEAD_DIM)

    def zmod(v):
        return lax.rem(v + nz, nz)

    def to_t(d):
        dx, dy = d // ny, d % ny
        return lax.rem(xh + dx, nxh) * ny + lax.rem(y + dy, ny)

    def from_t(d):
        dx, dy = d // ny, d % ny
        return lax.rem(xh + nxh - dx, nxh) * ny + lax.rem(y + ny - dy, ny)

    around = [ny * (1 - n % 2) + (n + 1) // 2 for n in range(nt - 1)]

    def near(k):
        a = 1 - xl if k // 2 else xl
        b = 1 - c if k % 2 else c
        return a, b

    def dev(zz, xx, cc, tt):
        return (zz * 4 + xx * 2 + cc, tt)

    counter = [0]
    pending = []

    def alloc(n):
        first = counter[0]
        counter[0] += n
        assert counter[0] <= r["n_sem"]
        return first

    def rcopy(src, dst, k, to):
        return pltpu.make_async_remote_copy(
            src_ref=src, dst_ref=dst, send_sem=ssem.at[k], recv_sem=rsem.at[k], device_id=to, device_id_type=MESH
        )

    right, left = dev(zmod(z + 1), xl, c, t), dev(zmod(z - 1), xl, c, t)
    cross = dev(z, 1 - xl, c, t)
    twin = dev(z, xl, 1 - c, t)

    def send(src, dst, k, to):
        copy = rcopy(src, dst, k, to)
        copy.start()
        pending.append(copy)

    def recv(dst, k):
        rcopy(dst, dst, k, twin).wait_recv()

    locals_ = [0]

    def lcopy(src, dst):
        copy = pltpu.make_async_copy(src, dst, lsem.at[locals_[0]])
        locals_[0] += 1
        copy.start()
        return copy

    n_right, n_left = nz // 2, (nz - 1) // 2

    class Ring:
        def __init__(self, slot):
            self.slot = slot
            self.kr, self.kl = alloc(n_right), alloc(n_left)

        def start(self):
            mine = self.slot(z)
            send(mine, mine, self.kr, right)
            if n_left:
                send(mine, mine, self.kl, left)

        def step(self, i):
            came = []
            ref = self.slot(zmod(z - i))
            recv(ref, self.kr + i - 1)
            came.append(zmod(z - i))
            if i < n_right:
                send(ref, ref, self.kr + i, right)
            if i <= n_left:
                ref = self.slot(zmod(z + i))
                recv(ref, self.kl + i - 1)
                came.append(zmod(z + i))
                if i < n_left:
                    send(ref, ref, self.kl + i, left)
            return came

    pall, a_ref, wg, d_out, w_v = r["pall"], r["a"], r["wg"], r["d_out"], r["w_v"]
    own_copies = [
        lcopy(patches, pall.at[t]),
        lcopy(
            text.at[:, :, pl.ds(pl.multiple_of(s4 * chunk, chunk), chunk)], a_ref.at[t, pl.ds(2 * xl, 2), c]
        ),
        lcopy(cot.at[c], d_out.at[c]),
    ]
    w_copies = []
    first = 0
    for name in ("wq", "wk", "wv"):
        n = r[name].shape[1]
        w_copies.append(lcopy(r[name], w_v.at[:, pl.ds(first, n)]))
        first += n
    inner_copy = lcopy(inner, r["inner_v"])
    outer_copies = [
        lcopy(outer.at[:, pl.ds(pl.multiple_of((tt * 4 + s4) * chunk, chunk), chunk)], r["outer_v"].at[tt])
        for tt in range(nt)
    ]

    barrier = pltpu.get_barrier_semaphore()
    peers = [dev(z, xl, c, to_t(d)) for d in range(1, nt)]
    peers += [dev(z, *near(k), t) for k in range(1, 4)] + [right, left]
    for peer in peers:
        pl.semaphore_signal(barrier, inc=1, device_id=peer, device_id_type=MESH)
    pl.semaphore_wait(barrier, len(peers))

    k_patch = alloc(nt)
    for d in range(1, nt):
        send(patches, pall.at[t], k_patch + d, dev(z, xl, c, to_t(d)))
    k_text = alloc(4)
    for k in range(1, 4):
        xx, cc = near(k)
        part = text.at[:, :, pl.ds(pl.multiple_of((xx * 2 + cc) * chunk, chunk), chunk)]
        send(part, a_ref.at[t, pl.ds(2 * xl, 2), c], k_text + k, dev(z, xx, cc, t))
    k_cot = alloc(1)
    send(cot.at[1 - c], d_out.at[c], k_cot, twin)

    r["gain_v"][...] = r["ngain"][...].reshape(r["gain_v"].shape)
    for copy in w_copies:
        copy.wait()
    for i in range(2):
        factor = column_of(r["gain_v"][pl.ds(sec * 2 + i, 1), :])[:, :1]
        rows_i = pl.ds(pl.multiple_of(z * 256 + i * 128, 128), 128)
        wg[rows_i, :] = (w_v[i * 128 : (i + 1) * 128, :].astype(F32) * factor).astype(BF)
    ring_w = Ring(lambda zz: wg.at[pl.ds(pl.multiple_of(zz * 256, 256), 256)])
    ring_w.start()

    pick, place, mask, kcol = r["pick"], r["place"], r["mask"], r["kcol"]
    total = nz * images
    slot = r["slot"][...].reshape(1, total)
    bits = seq.bit_length() - 1
    batch, pos = slot >> bits, slot & (seq - 1)
    key = ((pos >> 8) * plane + ((pos >> 7) & 1) * 256 + batch * 128 + (pos & 127)).astype(F32)
    for i in range(total // 128):
        kcol[i * 128 : (i + 1) * 128, :] = column_of(key[:, i * 128 : (i + 1) * 128])
    rank = jnp.sum(jnp.where(kcol[...][:, :1] < key, 1.0, 0.0), axis=0, keepdims=True)
    wide_rows = lax.broadcasted_iota(jnp.int32, (images, total), 0) + z * images
    pick[...] = jnp.where(rank == wide_rows.astype(F32), 1.0, 0.0).astype(BF)
    wide_rows = lax.broadcasted_iota(jnp.int32, (plane, total), 0) + z * plane
    stands = jnp.where(key == wide_rows.astype(F32), 1.0, 0.0).astype(BF)
    place[...] = dot_nt(stands, pick[...]).astype(BF)
    mask[...] = dot_nn(place[...], jnp.ones((images, chunk), BF))
    own_key = kcol[pl.ds(pl.multiple_of(z * images, images), images), :][:, :1]
    own_rank = jnp.sum(jnp.where(key < own_key, 1.0, 0.0), axis=1, keepdims=True)
    wanted, tsel, isel = r["wanted"], r["tsel"], r["isel"]
    wanted[...] = jnp.where(
        own_rank == lax.broadcasted_iota(jnp.int32, (images, total), 1).astype(F32), 1.0, 0.0
    ).astype(BF)
    earlier = jnp.where(
        lax.broadcasted_iota(jnp.int32, (128, 128), 0) < lax.broadcasted_iota(jnp.int32, (128, 128), 1), 1.0, 0.0
    ).astype(BF)

    def select(flags, count):
        nth = dot_nn(flags[:8].astype(BF), earlier)[:1]
        return jnp.where(
            nth == lax.broadcasted_iota(jnp.int32, (count, 128), 0).astype(F32), flags[:1], 0.0
        ).astype(BF)

    texts = 128 - rows
    for o in range(4):
        tsel[o] = select(1.0 - mask[o * 128 : (o + 1) * 128, :128].T, texts)
    isel[...] = select(mask[pl.ds(pl.multiple_of(s4 * 128, 128), 128), :128].T, rows)

    for copy in own_copies:
        copy.wait()

    for k in range(1, 4):
        xx, cc = near(k)
        recv(a_ref.at[t, pl.ds(2 * xx, 2), cc], k_text + k)
    k_a = alloc(nt)

    across_x = range(ny, nt, ny)
    for d in [*range(1, ny), *across_x]:
        send(a_ref.at[t], a_ref.at[t], k_a + d, dev(z, xl, c, to_t(d)))

    def text_on():
        for first in across_x:
            ref = a_ref.at[from_t(first)]
            recv(ref, k_a + first)
            for d in range(1, ny):
                send(ref, ref, k_a + first + d, dev(z, xl, c, to_t(d)))

    for d in range(1, nt):
        recv(pall.at[from_t(d)], k_patch + d)
    inner_copy.wait()
    vit = gain.shape[0]
    per = vit // pw
    hidden = None
    for piece in range(nt // per):
        wide = jnp.concatenate([pall[piece * per + i] for i in range(per)], axis=1).astype(F32)
        centre = jnp.mean(wide, axis=1, keepdims=True)
        shifted = wide - centre
        spread = jnp.mean(shifted * shifted, axis=1, keepdims=True)
        normed = (shifted * lax.rsqrt(spread + 1e-06) * gain[...].reshape(1, vit) + bias[...].reshape(1, vit)).astype(BF)
        term = dot_nn(normed, r["inner_v"][piece * vit : (piece + 1) * vit, :])
        hidden = term if hidden is None else hidden + term
    hidden = (0.5 * hidden * (1.0 + lax.erf(hidden * math.sqrt(0.5)))).astype(BF)

    class Gather:
        def __init__(self, slot_of):
            self.slot_of = slot_of
            self.k_cross, self.k_twin = alloc(1), alloc(2 * nz)
            mine = slot_of(z, xl, c)
            send(mine, mine, self.k_cross, cross)
            self.rings = [Ring(lambda zz: slot_of(zz, xl, c)), Ring(lambda zz: slot_of(zz, 1 - xl, c))]
            self.done = []
            self.rings[0].start()
            self.arrived(z, xl)

        def arrived(self, zz, xx):
            ref = self.slot_of(zz, xx, c)
            send(ref, ref, self.k_twin + len(self.done), twin)
            self.done.append((zz, xx))

        def crossed(self):
            recv(self.slot_of(z, 1 - xl, c), self.k_cross)
            self.rings[1].start()
            self.arrived(z, 1 - xl)

        def step(self, i):
            for ring, xx in zip(self.rings, (xl, 1 - xl)):
                for zz in ring.step(i):
                    self.arrived(zz, xx)

        def finish(self):
            for j, (zz, xx) in enumerate(self.done):
                recv(self.slot_of(zz, xx, 1 - c), self.k_twin + j)

    hall = r["hall"]
    hall[z, xl, c] = hidden
    ring_w.step(1)
    gather = Gather(lambda zz, xx, cc: hall.at[zz, xx, cc])
    gather.crossed()
    text_on()
    for i in range(1, n_right + 1):
        gather.step(i)
    gather.finish()
    if n_right > 2:
        ring_w.step(2)

    hp = dot_nn(pick[...], hall[...].reshape(total, hall.shape[4])).astype(BF)
    for copy in outer_copies:
        copy.wait()
    part_s, part_r, img = r["part_s"], r["part_r"], r["img"]
    k_part, k_img = alloc(nt), alloc(nt)
    for d in around:
        part_s[d] = dot_nn(hp, r["outer_v"][to_t(d)]).astype(BF)
        send(part_s.at[d], part_r.at[d], k_part + d, dev(z, xl, c, to_t(d)))
    mine = dot_nn(hp, r["outer_v"][t])
    for d in range(1, nt):
        recv(part_r.at[d], k_part + d)
        mine = mine + part_r[d].astype(F32)
    img[t] = mine.astype(BF)
    for d in around:
        send(img.at[t], img.at[t], k_img + d, dev(z, xl, c, to_t(d)))
    if n_right > 3:
        ring_w.step(3)

    xf, ss = r["xf"], r["ss"]

    def take(tt):
        placed = dot_nn(place[...], img[tt])
        x = jnp.where(mask[...] > 0.5, placed, a_ref[tt].reshape(plane, chunk).astype(F32))
        xf[:, pl.ds(pl.multiple_of(tt * chunk, chunk), chunk)] = x.astype(BF)
        x = x * x
        return x[:, :128] + x[:, 128:]

    ss[...] = take(t)

    def take_next(d, carry):
        @pl.when(lax.rem(d, ny) != 0)
        def _():
            recv(a_ref.at[from_t(d)], k_a + d)

        recv(img.at[from_t(d)], k_img + d)
        ss[...] += take(from_t(d))
        return carry

    lax.fori_loop(1, nt, take_next, 0)
    ss_all, inv = r["ss_all"], r["inv"]
    squares = jnp.sum(ss[...], axis=1, keepdims=True)
    for o in range(4):
        ss_all[s4, o] = row_tile(squares[o * 128 : (o + 1) * 128])
    k_ss, k_c = alloc(4), alloc(4)
    for k in range(1, 4):
        send(ss_all.at[s4], ss_all.at[s4], k_ss + k, dev(z, *near(k), t))
    ring_w.step(n_right)

    c_s, c_r, cn = r["c_s"], r["c_r"], r["cn"]
    def project(xx, cc):
        return dot_nn(xf[pl.ds(pl.multiple_of((xx * 2 + cc) * 128, 128), 128), :], wg[...])

    c_s[0] = project(1 - xl, 1 - c).astype(BF)
    send(c_s.at[0], c_r.at[0], k_c, twin)
    c_s[1] = project(xl, 1 - c).astype(BF)
    send(c_s.at[1], c_r.at[1], k_c + 1, twin)
    other = project(1 - xl, c)
    recv(c_r.at[0], k_c)
    c_s[2] = (other + c_r[0].astype(F32)).astype(BF)
    send(c_s.at[2], c_r.at[2], k_c + 2, cross)
    cn[...] = project(xl, c)
    for k in range(1, 4):
        xx, cc = near(k)
        recv(ss_all.at[xx * 2 + cc], k_ss + k)
    for o in range(4):
        tile = ss_all[0, o] + ss_all[1, o] + ss_all[2, o] + ss_all[3, o]
        inv[o] = column_of(lax.rsqrt(tile / width + 1e-06))
    projected = cn[...]
    for k in range(1, 3):
        recv(c_r.at[k], k_c + k)
        projected = projected + c_r[k].astype(F32)
    projected = projected * inv[s4][:, :1]
    cn[...] = projected
    heads = (projected.shape[1] - 2 * HEAD_DIM) // HEAD_DIM
    qs, kv, dos = r["qs"], r["kv"], r["dos"]
    for h in range(heads):
        qs[h] = projected[:, h * 128 : (h + 1) * 128].astype(BF)
    kv[z, xl] = projected[:, heads * 128 :].astype(BF)

    k_kv = alloc(1)
    send(kv.at[z, xl], kv.at[z, xl], k_kv, cross)
    rings = [Ring(lambda zz: kv.at[zz, xl]), Ring(lambda zz: kv.at[zz, 1 - xl])]
    rings[0].start()
    recv(kv.at[z, 1 - xl], k_kv)
    rings[1].start()
    own_s, own_r = r["own_s"], r["own_r"]
    k_own = alloc(nt)
    h_own = hall[z].reshape(images, hall.shape[4])
    for d in around:
        own_s[d] = dot_nn(h_own, r["outer_v"][to_t(d)]).astype(BF)
        send(own_s.at[d], own_r.at[d], k_own + d, dev(z, xl, c, to_t(d)))
    recv(d_out.at[1 - c], k_cot)
    for h in range(heads):
        dos[h] = d_out[:, :, h * 128 : (h + 1) * 128].reshape(128, 128)
    for i in range(1, n_right + 1):
        rings[0].step(i)
        rings[1].step(i)

    ph, ds, att, dq = r["ph"], r["ds"], r["att"], r["dq"]

    def head(h, carry):
        keys = kv[:, :, :, :128].reshape(seq, 128)
        values = kv[:, :, :, 128:].reshape(seq, 128)
        scores = dot_nt(qs[h], keys) * scale
        query_pos = z * 256 + xl * 128 + lax.broadcasted_iota(jnp.int32, (128, seq), 0)
        scores = jnp.where(lax.broadcasted_iota(jnp.int32, (128, seq), 1) <= query_pos, scores, -1e30)
        raw = jnp.exp(scores - jnp.max(scores, axis=1, keepdims=True))
        probs = raw * (1.0 / jnp.sum(raw, axis=1, keepdims=True))
        half = probs.astype(BF)
        ph[h] = half
        att[h] = dot_nn(half, values).astype(BF)
        grad_probs = dot_nt(dos[h], values)
        delta = jnp.sum(probs * grad_probs, axis=1, keepdims=True)
        grad = (probs * (grad_probs - delta)).astype(BF)
        ds[h] = grad
        dq[h] = (dot_nn(grad, keys) * scale).astype(BF)
        return carry

    lax.fori_loop(0, heads, head, 0, unroll=2)
    att_o, att_r = r["att_o"], r["att_r"]
    for h in range(heads):
        att_o[:, :, h * 128 : (h + 1) * 128] = att[h].reshape(2, 64, 128)
    k_att = alloc(1)
    send(att_o.at[1 - c], att_r, k_att, twin)

    sr, rr, sl, rl = r["sr"], r["rr"], r["sl"], r["rl"]
    kr, kl = alloc(2 * n_right), alloc(2 * max(n_left, 1))
    dx_s, dx_r = r["dx_s"], r["dx_r"]
    k_dx = alloc(1)

    def make(n, carry):
        zz, xx = lax.rem(z + n_right + lax.div(n, 2), nz), lax.rem(n, 2)
        lanes = pl.ds(pl.multiple_of((zz * 2 + xx) * 128, 128), 128)
        grad_keys = dot_tn(ds[:, :, lanes].reshape(heads * 128, 128), qs[...].reshape(heads * 128, 128))
        grad_values = dot_tn(ph[:, :, lanes].reshape(heads * 128, 128), dos[...].reshape(heads * 128, 128))
        dkv[zz, xx, :, :128] = grad_keys
        dkv[zz, xx, :, 128:] = grad_values
        return carry

    dkv = r["dkv"]
    lax.fori_loop(0, 4, make, 0)
    halves = ((0, 1 - xl), (1, xl))
    for i in range(n_right + 1):
        if i == 1:
            lax.fori_loop(4, 2 * nz, make, 0)
        for half, xx in halves:
            value = dkv[zmod(z + n_right - i), xx]
            if i:
                recv(rr.at[half, i - 1], kr + 2 * (i - 1) + half)
                value = value + rr[half, i - 1].astype(F32)
            if i < n_right:
                sr[half, i] = value.astype(BF)
                send(sr.at[half, i], rr.at[half, i], kr + 2 * i + half, right)
            elif half == 0:
                if n_left:
                    value = value + rl[half, n_left - 1].astype(F32)
                dx_s[...] = value.astype(BF)
                send(dx_s, dx_r, k_dx, cross)
            else:
                if n_left:
                    value = value + rl[half, n_left - 1].astype(F32)
                grad_kv = value
        for half, xx in halves:
            if n_left and i <= n_left:
                if i:
                    recv(rl.at[half, i - 1], kl + 2 * (i - 1) + half)
                if i < n_left:
                    value = dkv[zmod(z - n_left + i), xx]
                    if i:
                        value = value + rl[half, i - 1].astype(F32)
                    sl[half, i] = value.astype(BF)
                    send(sl.at[half, i], rl.at[half, i], kl + 2 * i + half, left)
    recv(dx_r, k_dx)
    grad_kv = grad_kv + dx_r[...].astype(F32)

    gg, inn, int_all = r["gg"], r["inn"], r["int_all"]
    pieces = [dq[h] for h in range(heads)]
    pieces += [(grad_kv[:, :128] * scale).astype(BF), grad_kv[:, 128:].astype(BF)]
    grads = jnp.concatenate(pieces, axis=1)
    inn_tile = row_tile(jnp.sum(grads.astype(F32) * cn[...], axis=1, keepdims=True))
    inn[s4] = inn_tile
    marks = isel[...].astype(F32)
    beside = (
        jnp.sum(marks * inv[s4].T[:1], axis=1, keepdims=True),
        jnp.sum(marks * inn_tile[:1], axis=1, keepdims=True),
    )
    lane = lax.broadcasted_iota(jnp.int32, (rows, 128), 1)
    extra = jnp.zeros((rows, 128), F32)
    for n, value in enumerate(beside):
        for m in range(3):
            part = value.astype(BF).astype(F32)
            extra = jnp.where(lane == 3 * n + m, part, extra)
            value = value - part
    rall = r["rall"]
    rall[z, xl, c] = jnp.concatenate([dot_nn(isel[...], grads).astype(BF), extra.astype(BF)], axis=1)
    gather = Gather(lambda zz, xx, cc: rall.at[zz, xx, cc])

    gg[s4] = dot_nn(tsel[s4], grads).astype(BF)
    k_gg, k_inn = alloc(3), alloc(4)
    send(gg.at[s4], gg.at[s4], k_gg, twin)
    send(gg.at[s4], gg.at[s4], k_gg + 1, cross)
    for k in range(1, 4):
        send(inn.at[s4], inn.at[s4], k_inn + k, dev(z, *near(k), t))
    k_int, k_back, k_int2, k_back2 = alloc(nt), alloc(2 * nt), alloc(nt), alloc(nt)

    bs, br, bo = r["bs"], r["br"], r["bo"]
    depth_all = gg.shape[2]

    def back(half, xx):
        def one(tt):
            lines = gg[pl.ds(2 * xx, 2)].reshape(2 * texts, depth_all)
            return dot_nt(lines, wg[pl.ds(pl.multiple_of(tt * chunk, chunk), chunk), :])

        def step(n, carry):
            d = ny * (1 - n % 2) + (n + 1) // 2
            tt = to_t(d)
            bs[d, xx] = one(tt).astype(BF)
            rcopy(bs.at[d, xx], br.at[d, xx], k_back + 2 * d + half, dev(z, xl, c, tt)).start()
            return carry

        lax.fori_loop(0, nt - 1, step, 0)
        for d in range(1, nt):
            pending.append(rcopy(bs.at[d, xx], br.at[d, xx], k_back + 2 * d + half, dev(z, xl, c, to_t(d))))
        return one

    recv(gg.at[xl * 2 + 1 - c], k_gg)
    near_half = back(0, xl)
    gather.crossed()
    across, corner = gg.at[(1 - xl) * 2 + c], gg.at[(1 - xl) * 2 + 1 - c]
    recv(across, k_gg + 1)
    send(across, across, k_gg + 2, twin)
    for k in range(1, 4):
        xx, cc = near(k)
        recv(inn.at[xx * 2 + cc], k_inn + k)
    int_all[t] = inn[...]
    for d in range(1, nt):
        send(int_all.at[t], int_all.at[t], k_int + d, dev(z, xl, c, to_t(d)))
    recv(corner, k_gg + 2)
    far_half = back(1, 1 - xl)
    for i in range(1, n_right + 1):
        gather.step(i)
        if i == 1:
            bo[xl] = near_half(t)
            bo[1 - xl] = far_half(t)
            own_x = dot_nn(h_own, r["outer_v"][t])
            for d in range(1, nt):
                recv(own_r.at[d], k_own + d)
                own_x = own_x + own_r[d].astype(F32)
            own_x = own_x.astype(BF).astype(F32)
    gather.finish()

    routed = dot_nn(wanted[...], rall[...].reshape(total, rall.shape[4]))
    inv_row = routed[:, depth_all : depth_all + 1] + routed[:, depth_all + 1 : depth_all + 2]
    inv_row = inv_row + routed[:, depth_all + 2 : depth_all + 3]
    inn_row = routed[:, depth_all + 3 : depth_all + 4] + routed[:, depth_all + 4 : depth_all + 5]
    inn_row = inn_row + routed[:, depth_all + 5 : depth_all + 6]
    routed = routed[:, :depth_all].astype(BF)
    int_own = r["int_own"]
    int_own[t] = row_tile(inn_row)
    bs2, br2 = r["bs2"], r["br2"]
    for d in around:
        bs2[d] = dot_nt(routed, wg[pl.ds(pl.multiple_of(to_t(d) * chunk, chunk), chunk), :]).astype(BF)
        send(bs2.at[d], br2.at[d], k_back2 + d, dev(z, xl, c, to_t(d)))
        send(int_own.at[t], int_own.at[t], k_int2 + d, dev(z, xl, c, to_t(d)))
    own_back = dot_nt(routed, wg[pl.ds(pl.multiple_of(t * chunk, chunk), chunk), :])

    for d in range(1, nt):
        recv(int_all.at[from_t(d)], k_int + d)
    for d in range(1, nt):
        for half, xx in ((0, xl), (1, 1 - xl)):
            recv(br.at[d, xx], k_back + 2 * d + half)
        bo[...] += br[d].astype(F32)
    gt_s, gt_r = r["gt_s"], r["gt_r"]
    for o in range(4):
        tile = int_all[0, o]
        for d in range(1, nt):
            tile = tile + int_all[d, o]
        marks = tsel[o].astype(F32)
        inv_o = jnp.sum(marks * inv[o].T[:1], axis=1, keepdims=True)
        inn_o = jnp.sum(marks * tile[:1], axis=1, keepdims=True)
        x = dot_nn(tsel[o], xf[o * 128 : (o + 1) * 128, pl.ds(pl.multiple_of(t * chunk, chunk), chunk)])
        grad = inv_o * bo[o // 2, o % 2 * texts : (o % 2 + 1) * texts, :] - x * (inv_o * inv_o * inn_o / width)
        gt_s[o] = dot_tn(tsel[o], grad.astype(BF)).astype(BF).reshape(2, 64, chunk)
    k_gt, k_gr = alloc(4), alloc(4)
    for k in range(1, 4):
        xx, cc = near(k)
        send(gt_s.at[pl.ds(2 * xx, 2), cc], gt_r.at[s4], k_gt + k, dev(z, xx, cc, t))
    gt_r[s4] = gt_s[pl.ds(2 * xl, 2), c]

    for d in range(1, nt):
        recv(int_own.at[from_t(d)], k_int2 + d)
        recv(br2.at[d], k_back2 + d)
        own_back = own_back + br2[d].astype(F32)
    tile = int_own[0]
    for d in range(1, nt):
        tile = tile + int_own[d]
    grad = inv_row * own_back - own_x * (inv_row * inv_row * column_of(tile)[:, :1] / width)
    gr_s, gr_r = r["gr_s"], r["gr_r"]
    gr_s[...] = grad.astype(BF).reshape(4, rows, chunk)
    for k in range(1, 4):
        xx, cc = near(k)
        send(gr_s.at[xx * 2 + cc], gr_r.at[s4], k_gr + k, dev(z, xx, cc, t))
    gr_r[s4] = gr_s[s4]
    for k in range(1, 4):
        xx, cc = near(k)
        recv(gt_r.at[xx * 2 + cc], k_gt + k)
    for o in range(4):
        r["gtext"][:, :, o * chunk : (o + 1) * chunk] = gt_r[o]
    for k in range(1, 4):
        xx, cc = near(k)
        recv(gr_r.at[xx * 2 + cc], k_gr + k)
    for o in range(4):
        r["gimage"][:, o * chunk : (o + 1) * chunk] = gr_r[o]
    recv(att_r, k_att)
    r["attended"][c] = att_o[c]
    r["attended"][1 - c] = att_r[...]
    for copy in pending:
        copy.wait_send()


def per_device(
    patches,
    merge_gain,
    merge_bias,
    merge_inner,
    merge_outer,
    slot_target,
    text_embed,
    norm_gain,
    query_weight,
    key_weight,
    value_weight,
    attn_cotangent,
):
    nsec, nt = lax.axis_size("sec"), lax.axis_size("tp")
    nz, ny = nsec // 4, max(nt // 2, 1)
    rows, pw = patches.shape
    hid = merge_inner.shape[1]
    micro, tok, feat = text_embed.shape
    chunk = feat // 4
    seq = tok * nsec
    images = 4 * rows
    total = nz * images
    depth = query_weight.shape[0]
    heads = query_weight.shape[1] // HEAD_DIM
    cols = (heads + 2) * HEAD_DIM
    plane = 512

    vmem, anyspace = pl.BlockSpec(memory_space=pltpu.VMEM), pl.BlockSpec(memory_space=pl.ANY)
    n_right, n_left = nz // 2, max((nz - 1) // 2, 1)
    n_sem = 320
    ins = ["patches", "gain", "bias", "inner", "outer", "slot", "ngain", "text", "wq", "wk", "wv", "cot"]
    outs = ["attended", "gtext", "gimage"]
    scratch = dict(
        pall=((nt, rows, pw), BF),
        inner_v=(merge_inner.shape, BF),
        outer_v=((nt, hid, chunk), BF),
        a=((nt, 4, 2, tok, chunk), BF),
        wg=((nz * depth, cols), BF),
        d_out=((2, tok, heads * HEAD_DIM), BF),
        w_v=((depth, cols), BF),
        gain_v=((depth * nsec // 128, 128), F32),
        kcol=((total, 128), F32),
        wanted=((images, total), BF),
        tsel=((4, 128 - rows, 128), BF),
        isel=((rows, 128), BF),
        own_s=((nt, images, chunk), BF),
        own_r=((nt, images, chunk), BF),
        int_own=((nt, 8, 128), F32),
        bs2=((nt, images, chunk), BF),
        br2=((nt, images, chunk), BF),
        gr_s=((4, rows, chunk), BF),
        gr_r=((4, rows, chunk), BF),
        hall=((nz, 2, 2, rows, hid), BF),
        pick=((images, total), BF),
        place=((plane, images), BF),
        mask=((plane, chunk), F32),
        part_s=((nt, images, chunk), BF),
        part_r=((nt, images, chunk), BF),
        img=((nt, images, chunk), BF),
        xf=((plane, nt * chunk), BF),
        ss=((plane, 128), F32),
        ss_all=((4, 4, 8, 128), F32),
        inv=((4, 128, 128), F32),
        c_s=((3, 128, cols), BF),
        c_r=((3, 128, cols), BF),
        cn=((128, cols), F32),
        qs=((heads, 128, 128), BF),
        kv=((nz, 2, 128, 256), BF),
        dos=((heads, 128, 128), BF),
        ph=((heads, 128, seq), BF),
        ds=((heads, 128, seq), BF),
        att=((heads, 128, 128), BF),
        dq=((heads, 128, 128), BF),
        att_o=((2, tok, heads * HEAD_DIM), BF),
        att_r=((tok, heads * HEAD_DIM), BF),
        sr=((2, n_right, 128, 256), BF),
        rr=((2, n_right, 128, 256), BF),
        sl=((2, n_left, 128, 256), BF),
        rl=((2, n_left, 128, 256), BF),
        dkv=((nz, 2, 128, 256), F32),
        dx_s=((128, 256), BF),
        dx_r=((128, 256), BF),
        gg=((4, 128 - rows, cols), BF),
        inn=((4, 8, 128), F32),
        int_all=((nt, 4, 8, 128), F32),
        bs=((nt, 2, 2 * (128 - rows), chunk), BF),
        br=((nt, 2, 2 * (128 - rows), chunk), BF),
        bo=((2, 2 * (128 - rows), chunk), F32),
        gt_s=((4, 2, tok, chunk), BF),
        gt_r=((4, 2, tok, chunk), BF),
        rall=((nz, 2, 2, rows, cols + 128), BF),
    )
    names = ins + outs + list(scratch) + ["ssem", "rsem", "lsem", "n_sem"]
    call = pl.pallas_call(
        lambda *refs: kernel(nz, nt, ny, names, *refs, n_sem),
        out_shape=(
            jax.ShapeDtypeStruct((micro, tok, heads * HEAD_DIM), BF),
            jax.ShapeDtypeStruct((micro, tok, feat), BF),
            jax.ShapeDtypeStruct((rows, feat), BF),
        ),
        in_specs=[vmem if n in ("gain", "bias", "slot", "ngain") else anyspace for n in ins],
        out_specs=(vmem,) * 3,
        scratch_shapes=[pltpu.VMEM(shape, dtype) for shape, dtype in scratch.values()]
        + [
            pltpu.SemaphoreType.DMA((n_sem,)),
            pltpu.SemaphoreType.DMA((n_sem,)),
            pltpu.SemaphoreType.DMA((24,)),
        ],
        compiler_params=pltpu.CompilerParams(
            collective_id=0, has_side_effects=True, vmem_limit_bytes=56 * 1024 * 1024
        ),
        name="merged_step",
    )
    return call(
        patches,
        merge_gain,
        merge_bias,
        merge_inner,
        merge_outer,
        slot_target,
        norm_gain,
        text_embed,
        query_weight,
        key_weight,
        value_weight,
        attn_cotangent,
    )


def solution(mesh):
    return jax.shard_map(
        per_device,
        mesh=mesh,
        in_specs=(
            P("sec", "tp"),
            P(),
            P(),
            P(None, "tp"),
            P("tp", None),
            P(),
            P(None, "sec", "tp"),
            P(),
            P("sec", "tp"),
            P("sec", "tp"),
            P("sec", "tp"),
            P(None, "sec", "tp"),
        ),
        out_specs=(P(None, "sec", "tp"), P(None, "sec", "tp"), P("sec", "tp")),
        check_vma=False,
    )
```

```python
import functools
import math

import jax
import jax.numpy as jnp
from jax import lax
from jax.experimental import pallas as pl
from jax.experimental.pallas import tpu as pltpu
from jax.sharding import PartitionSpec as P

HEAD_DIM = 128
BF = jnp.bfloat16
F32 = jnp.float32
MESH = pl.DeviceIdType.MESH


def dot_nn(a, b):
    return jnp.dot(a, b, preferred_element_type=F32)


def dot_nt(a, b):
    return lax.dot_general(a, b, (((1,), (1,)), ((), ())), preferred_element_type=F32)


def dot_tn(a, b):
    return lax.dot_general(a, b, (((0,), (0,)), ((), ())), preferred_element_type=F32)


def row_tile(column):
    return jnp.broadcast_to(column, (128, 128)).T[:8]


def column_of(tile):
    return jnp.broadcast_to(tile[0:1, :], (128, 128)).T


def kernel(nz, nt, ny, names, *refs):
    r = dict(zip(names, refs))
    patches, gain, bias, inner, outer = (r[n] for n in ("patches", "gain", "bias", "inner", "outer"))
    text, cot = r["text"], r["cot"]
    ssem, rsem, lsem = r["ssem"], r["rsem"], r["lsem"]
    sec, t = lax.axis_index("sec"), lax.axis_index("tp")
    z, s4 = lax.div(sec, 4), lax.rem(sec, 4)
    xl, c = lax.div(s4, 2), lax.rem(s4, 2)
    nxh = nt // ny
    xh, y = lax.div(t, ny), lax.rem(t, ny)
    rows, pw = patches.shape
    chunk = text.shape[2] // 4
    plane = 4 * 128
    images = 4 * rows
    width = text.shape[2] * nt
    seq = nz * 256
    scale = 1.0 / math.sqrt(HEAD_DIM)

    def zmod(v):
        return lax.rem(v + nz, nz)

    def to_t(d):
        dx, dy = d // ny, d % ny
        return lax.rem(xh + dx, nxh) * ny + lax.rem(y + dy, ny)

    def from_t(d):
        dx, dy = d // ny, d % ny
        return lax.rem(xh + nxh - dx, nxh) * ny + lax.rem(y + ny - dy, ny)

    around = [ny * (1 - n % 2) + (n + 1) // 2 for n in range(nt - 1)]

    def near(k):
        a = 1 - xl if k // 2 else xl
        b = 1 - c if k % 2 else c
        return a, b

    def dev(zz, xx, cc, tt):
        return (zz * 4 + xx * 2 + cc, tt)

    counter = [0]
    pending = []

    def alloc(n):
        first = counter[0]
        counter[0] += n
        assert counter[0] <= r["n_sem"]
        return first

    def rcopy(src, dst, k, to):
        return pltpu.make_async_remote_copy(
            src_ref=src, dst_ref=dst, send_sem=ssem.at[k], recv_sem=rsem.at[k], device_id=to, device_id_type=MESH
        )

    right, left = dev(zmod(z + 1), xl, c, t), dev(zmod(z - 1), xl, c, t)
    cross = dev(z, 1 - xl, c, t)
    twin = dev(z, xl, 1 - c, t)

    def send(src, dst, k, to):
        copy = rcopy(src, dst, k, to)
        copy.start()
        pending.append(copy)

    def recv(dst, k):
        rcopy(dst, dst, k, twin).wait_recv()

    locals_ = [0]

    def lcopy(src, dst):
        copy = pltpu.make_async_copy(src, dst, lsem.at[locals_[0]])
        locals_[0] += 1
        copy.start()
        return copy

    n_right, n_left = nz // 2, (nz - 1) // 2

    class Ring:
        def __init__(self, slot):
            self.slot = slot
            self.kr, self.kl = alloc(n_right), alloc(n_left)

        def start(self):
            mine = self.slot(z)
            send(mine, mine, self.kr, right)
            if n_left:
                send(mine, mine, self.kl, left)

        def step(self, i):
            came = []
            ref = self.slot(zmod(z - i))
            recv(ref, self.kr + i - 1)
            came.append(zmod(z - i))
            if i < n_right:
                send(ref, ref, self.kr + i, right)
            if i <= n_left:
                ref = self.slot(zmod(z + i))
                recv(ref, self.kl + i - 1)
                came.append(zmod(z + i))
                if i < n_left:
                    send(ref, ref, self.kl + i, left)
            return came

    pall, a_ref, wg, d_out, w_v = r["pall"], r["a"], r["wg"], r["d_out"], r["w_v"]
    own_copies = [
        lcopy(patches, pall.at[t]),
        lcopy(
            text.at[:, :, pl.ds(pl.multiple_of(s4 * chunk, chunk), chunk)], a_ref.at[t, pl.ds(2 * xl, 2), c]
        ),
        lcopy(cot.at[c], d_out.at[c]),
    ]
    w_copies = []
    first = 0
    for name in ("wq", "wk", "wv"):
        n = r[name].shape[1]
        w_copies.append(lcopy(r[name], w_v.at[:, pl.ds(first, n)]))
        first += n
    inner_copy = lcopy(inner, r["inner_v"])
    outer_copies = [
        lcopy(outer.at[:, pl.ds(pl.multiple_of((tt * 4 + s4) * chunk, chunk), chunk)], r["outer_v"].at[tt])
        for tt in range(nt)
    ]

    barrier = pltpu.get_barrier_semaphore()
    peers = [dev(z, xl, c, to_t(d)) for d in range(1, nt)]
    peers += [dev(z, *near(k), t) for k in range(1, 4)] + [right, left]
    for peer in peers:
        pl.semaphore_signal(barrier, inc=1, device_id=peer, device_id_type=MESH)
    pl.semaphore_wait(barrier, len(peers))

    k_patch = alloc(nt)
    for d in range(1, nt):
        send(patches, pall.at[t], k_patch + d, dev(z, xl, c, to_t(d)))
    k_text = alloc(4)
    for k in range(1, 4):
        xx, cc = near(k)
        part = text.at[:, :, pl.ds(pl.multiple_of((xx * 2 + cc) * chunk, chunk), chunk)]
        send(part, a_ref.at[t, pl.ds(2 * xl, 2), c], k_text + k, dev(z, xx, cc, t))
    k_cot = alloc(1)
    send(cot.at[1 - c], d_out.at[c], k_cot, twin)

    r["gain_v"][...] = r["ngain"][...].reshape(r["gain_v"].shape)
    for copy in w_copies:
        copy.wait()
    for i in range(2):
        factor = column_of(r["gain_v"][pl.ds(sec * 2 + i, 1), :])[:, :1]
        rows_i = pl.ds(pl.multiple_of(z * 256 + i * 128, 128), 128)
        wg[rows_i, :] = (w_v[i * 128 : (i + 1) * 128, :].astype(F32) * factor).astype(BF)
    ring_w = Ring(lambda zz: wg.at[pl.ds(pl.multiple_of(zz * 256, 256), 256)])
    ring_w.start()

    pick, place, mask, kcol = r["pick"], r["place"], r["mask"], r["kcol"]
    total = nz * images
    slot = r["slot"][...].reshape(1, total)
    bits = seq.bit_length() - 1
    batch, pos = slot >> bits, slot & (seq - 1)
    key = ((pos >> 8) * plane + ((pos >> 7) & 1) * 256 + batch * 128 + (pos & 127)).astype(F32)
    for i in range(total // 128):
        kcol[i * 128 : (i + 1) * 128, :] = column_of(key[:, i * 128 : (i + 1) * 128])
    rank = jnp.sum(jnp.where(kcol[...][:, :1] < key, 1.0, 0.0), axis=0, keepdims=True)
    wide_rows = lax.broadcasted_iota(jnp.int32, (images, total), 0) + z * images
    pick[...] = jnp.where(rank == wide_rows.astype(F32), 1.0, 0.0).astype(BF)
    wide_rows = lax.broadcasted_iota(jnp.int32, (plane, total), 0) + z * plane
    stands = jnp.where(key == wide_rows.astype(F32), 1.0, 0.0).astype(BF)
    place[...] = dot_nt(stands, pick[...]).astype(BF)
    mask[...] = dot_nn(place[...], jnp.ones((images, chunk), BF))
    own_key = kcol[pl.ds(pl.multiple_of(z * images, images), images), :][:, :1]
    own_rank = jnp.sum(jnp.where(key < own_key, 1.0, 0.0), axis=1, keepdims=True)
    wanted, tsel, isel = r["wanted"], r["tsel"], r["isel"]
    wanted[...] = jnp.where(
        own_rank == lax.broadcasted_iota(jnp.int32, (images, total), 1).astype(F32), 1.0, 0.0
    ).astype(BF)
    earlier = jnp.where(
        lax.broadcasted_iota(jnp.int32, (128, 128), 0) < lax.broadcasted_iota(jnp.int32, (128, 128), 1), 1.0, 0.0
    ).astype(BF)

    def select(flags, count):
        nth = dot_nn(flags[:8].astype(BF), earlier)[:1]
        return jnp.where(
            nth == lax.broadcasted_iota(jnp.int32, (count, 128), 0).astype(F32), flags[:1], 0.0
        ).astype(BF)

    texts = 128 - rows
    for o in range(4):
        tsel[o] = select(1.0 - mask[o * 128 : (o + 1) * 128, :128].T, texts)
    isel[...] = select(mask[pl.ds(pl.multiple_of(s4 * 128, 128), 128), :128].T, rows)

    for copy in own_copies:
        copy.wait()

    for k in range(1, 4):
        xx, cc = near(k)
        recv(a_ref.at[t, pl.ds(2 * xx, 2), cc], k_text + k)
    k_a = alloc(nt)

    across_x = range(ny, nt, ny)
    for d in [*range(1, ny), *across_x]:
        send(a_ref.at[t], a_ref.at[t], k_a + d, dev(z, xl, c, to_t(d)))

    def text_on():
        for first in across_x:
            ref = a_ref.at[from_t(first)]
            recv(ref, k_a + first)
            for d in range(1, ny):
                send(ref, ref, k_a + first + d, dev(z, xl, c, to_t(d)))

    for d in range(1, nt):
        recv(pall.at[from_t(d)], k_patch + d)
    inner_copy.wait()
    vit = gain.shape[0]
    per = vit // pw
    hidden = None
    for piece in range(nt // per):
        wide = jnp.concatenate([pall[piece * per + i] for i in range(per)], axis=1).astype(F32)
        centre = jnp.mean(wide, axis=1, keepdims=True)
        shifted = wide - centre
        spread = jnp.mean(shifted * shifted, axis=1, keepdims=True)
        normed = (shifted * lax.rsqrt(spread + 1e-06) * gain[...].reshape(1, vit) + bias[...].reshape(1, vit)).astype(BF)
        term = dot_nn(normed, r["inner_v"][piece * vit : (piece + 1) * vit, :])
        hidden = term if hidden is None else hidden + term
    hidden = (0.5 * hidden * (1.0 + lax.erf(hidden * math.sqrt(0.5)))).astype(BF)

    class Gather:
        def __init__(self, slot_of):
            self.slot_of = slot_of
            self.k_cross, self.k_twin = alloc(1), alloc(2 * nz)
            mine = slot_of(z, xl, c)
            send(mine, mine, self.k_cross, cross)
            self.rings = [Ring(lambda zz: slot_of(zz, xl, c)), Ring(lambda zz: slot_of(zz, 1 - xl, c))]
            self.done = []
            self.rings[0].start()
            self.arrived(z, xl)

        def arrived(self, zz, xx):
            ref = self.slot_of(zz, xx, c)
            send(ref, ref, self.k_twin + len(self.done), twin)
            self.done.append((zz, xx))

        def crossed(self):
            recv(self.slot_of(z, 1 - xl, c), self.k_cross)
            self.rings[1].start()
            self.arrived(z, 1 - xl)

        def step(self, i):
            for ring, xx in zip(self.rings, (xl, 1 - xl)):
                for zz in ring.step(i):
                    self.arrived(zz, xx)

        def finish(self):
            for j, (zz, xx) in enumerate(self.done):
                recv(self.slot_of(zz, xx, 1 - c), self.k_twin + j)

    hall = r["hall"]
    hall[z, xl, c] = hidden
    ring_w.step(1)
    gather = Gather(lambda zz, xx, cc: hall.at[zz, xx, cc])
    gather.crossed()
    text_on()
    for i in range(1, n_right + 1):
        gather.step(i)
    gather.finish()
    if n_right > 2:
        ring_w.step(2)

    hp = dot_nn(pick[...], hall[...].reshape(total, hall.shape[4])).astype(BF)
    for copy in outer_copies:
        copy.wait()
    part_s, part_r, img = r["part_s"], r["part_r"], r["img"]
    k_part, k_img = alloc(nt), alloc(nt)
    for d in around:
        part_s[d] = dot_nn(hp, r["outer_v"][to_t(d)]).astype(BF)
        send(part_s.at[d], part_r.at[d], k_part + d, dev(z, xl, c, to_t(d)))
    mine = dot_nn(hp, r["outer_v"][t])
    for d in range(1, nt):
        recv(part_r.at[d], k_part + d)
        mine = mine + part_r[d].astype(F32)
    img[t] = mine.astype(BF)
    for d in around:
        send(img.at[t], img.at[t], k_img + d, dev(z, xl, c, to_t(d)))
    if n_right > 3:
        ring_w.step(3)

    xf, ss = r["xf"], r["ss"]

    def take(tt):
        placed = dot_nn(place[...], img[tt])
        x = jnp.where(mask[...] > 0.5, placed, a_ref[tt].reshape(plane, chunk).astype(F32))
        xf[:, pl.ds(pl.multiple_of(tt * chunk, chunk), chunk)] = x.astype(BF)
        x = x * x
        return x[:, :128] + x[:, 128:]

    ss[...] = take(t)

    def take_next(d, carry):
        @pl.when(lax.rem(d, ny) != 0)
        def _():
            recv(a_ref.at[from_t(d)], k_a + d)

        recv(img.at[from_t(d)], k_img + d)
        ss[...] += take(from_t(d))
        return carry

    lax.fori_loop(1, nt, take_next, 0)
    ss_all, inv = r["ss_all"], r["inv"]
    squares = jnp.sum(ss[...], axis=1, keepdims=True)
    for o in range(4):
        ss_all[s4, o] = row_tile(squares[o * 128 : (o + 1) * 128])
    k_ss, k_c = alloc(4), alloc(4)
    for k in range(1, 4):
        send(ss_all.at[s4], ss_all.at[s4], k_ss + k, dev(z, *near(k), t))
    ring_w.step(n_right)

    c_s, c_r, cn = r["c_s"], r["c_r"], r["cn"]
    def project(xx, cc):
        return dot_nn(xf[pl.ds(pl.multiple_of((xx * 2 + cc) * 128, 128), 128), :], wg[...])

    c_s[0] = project(1 - xl, 1 - c).astype(BF)
    send(c_s.at[0], c_r.at[0], k_c, twin)
    c_s[1] = project(xl, 1 - c).astype(BF)
    send(c_s.at[1], c_r.at[1], k_c + 1, twin)
    other = project(1 - xl, c)
    recv(c_r.at[0], k_c)
    c_s[2] = (other + c_r[0].astype(F32)).astype(BF)
    send(c_s.at[2], c_r.at[2], k_c + 2, cross)
    cn[...] = project(xl, c)
    for k in range(1, 4):
        xx, cc = near(k)
        recv(ss_all.at[xx * 2 + cc], k_ss + k)
    for o in range(4):
        tile = ss_all[0, o] + ss_all[1, o] + ss_all[2, o] + ss_all[3, o]
        inv[o] = column_of(lax.rsqrt(tile / width + 1e-06))
    projected = cn[...]
    for k in range(1, 3):
        recv(c_r.at[k], k_c + k)
        projected = projected + c_r[k].astype(F32)
    projected = projected * inv[s4][:, :1]
    cn[...] = projected
    heads = (projected.shape[1] - 2 * HEAD_DIM) // HEAD_DIM
    qs, kv, dos = r["qs"], r["kv"], r["dos"]
    for h in range(heads):
        qs[h] = projected[:, h * 128 : (h + 1) * 128].astype(BF)
    kv[z, xl] = projected[:, heads * 128 :].astype(BF)

    k_kv = alloc(1)
    send(kv.at[z, xl], kv.at[z, xl], k_kv, cross)
    rings = [Ring(lambda zz: kv.at[zz, xl]), Ring(lambda zz: kv.at[zz, 1 - xl])]
    rings[0].start()
    recv(kv.at[z, 1 - xl], k_kv)
    rings[1].start()
    own_s, own_r = r["own_s"], r["own_r"]
    k_own = alloc(nt)
    h_own = hall[z].reshape(images, hall.shape[4])
    for d in around:
        own_s[d] = dot_nn(h_own, r["outer_v"][to_t(d)]).astype(BF)
        send(own_s.at[d], own_r.at[d], k_own + d, dev(z, xl, c, to_t(d)))
    recv(d_out.at[1 - c], k_cot)
    for h in range(heads):
        dos[h] = d_out[:, :, h * 128 : (h + 1) * 128].reshape(128, 128)
    for i in range(1, n_right + 1):
        rings[0].step(i)
        rings[1].step(i)

    ph, ds, att, dq = r["ph"], r["ds"], r["att"], r["dq"]

    def head(h, carry):
        keys = kv[:, :, :, :128].reshape(seq, 128)
        values = kv[:, :, :, 128:].reshape(seq, 128)
        scores = dot_nt(qs[h], keys) * scale
        query_pos = z * 256 + xl * 128 + lax.broadcasted_iota(jnp.int32, (128, seq), 0)
        scores = jnp.where(lax.broadcasted_iota(jnp.int32, (128, seq), 1) <= query_pos, scores, -1e30)
        raw = jnp.exp(scores - jnp.max(scores, axis=1, keepdims=True))
        probs = raw * (1.0 / jnp.sum(raw, axis=1, keepdims=True))
        half = probs.astype(BF)
        ph[h] = half
        att[h] = dot_nn(half, values).astype(BF)
        grad_probs = dot_nt(dos[h], values)
        delta = jnp.sum(probs * grad_probs, axis=1, keepdims=True)
        grad = (probs * (grad_probs - delta)).astype(BF)
        ds[h] = grad
        dq[h] = (dot_nn(grad, keys) * scale).astype(BF)
        return carry

    lax.fori_loop(0, heads, head, 0, unroll=4)
    att_o, att_r = r["att_o"], r["att_r"]
    for h in range(heads):
        att_o[:, :, h * 128 : (h + 1) * 128] = att[h].reshape(2, 64, 128)
    k_att = alloc(1)
    send(att_o.at[1 - c], att_r, k_att, twin)

    sr, rr, sl, rl = r["sr"], r["rr"], r["sl"], r["rl"]
    kr, kl = alloc(2 * n_right), alloc(2 * max(n_left, 1))
    dx_s, dx_r = r["dx_s"], r["dx_r"]
    k_dx = alloc(1)

    def make(n, carry):
        zz, xx = lax.rem(z + n_right + lax.div(n, 2), nz), lax.rem(n, 2)
        lanes = pl.ds(pl.multiple_of((zz * 2 + xx) * 128, 128), 128)
        grad_keys = dot_tn(ds[:, :, lanes].reshape(heads * 128, 128), qs[...].reshape(heads * 128, 128))
        grad_values = dot_tn(ph[:, :, lanes].reshape(heads * 128, 128), dos[...].reshape(heads * 128, 128))
        dkv[zz, xx, :, :128] = grad_keys
        dkv[zz, xx, :, 128:] = grad_values
        return carry

    dkv = r["dkv"]
    lax.fori_loop(0, 4, make, 0)
    halves = ((0, 1 - xl), (1, xl))
    for i in range(n_right + 1):
        if i == 1:
            lax.fori_loop(4, 2 * nz, make, 0)
        for half, xx in halves:
            value = dkv[zmod(z + n_right - i), xx]
            if i:
                recv(rr.at[half, i - 1], kr + 2 * (i - 1) + half)
                value = value + rr[half, i - 1].astype(F32)
            if i < n_right:
                sr[half, i] = value.astype(BF)
                send(sr.at[half, i], rr.at[half, i], kr + 2 * i + half, right)
            elif half == 0:
                if n_left:
                    value = value + rl[half, n_left - 1].astype(F32)
                dx_s[...] = value.astype(BF)
                send(dx_s, dx_r, k_dx, cross)
            else:
                if n_left:
                    value = value + rl[half, n_left - 1].astype(F32)
                grad_kv = value
        for half, xx in halves:
            if n_left and i <= n_left:
                if i:
                    recv(rl.at[half, i - 1], kl + 2 * (i - 1) + half)
                if i < n_left:
                    value = dkv[zmod(z - n_left + i), xx]
                    if i:
                        value = value + rl[half, i - 1].astype(F32)
                    sl[half, i] = value.astype(BF)
                    send(sl.at[half, i], rl.at[half, i], kl + 2 * i + half, left)
    recv(dx_r, k_dx)
    grad_kv = grad_kv + dx_r[...].astype(F32)

    gg, inn, int_all = r["gg"], r["inn"], r["int_all"]
    pieces = [dq[h] for h in range(heads)]
    pieces += [(grad_kv[:, :128] * scale).astype(BF), grad_kv[:, 128:].astype(BF)]
    grads = jnp.concatenate(pieces, axis=1)
    inn_tile = row_tile(jnp.sum(grads.astype(F32) * cn[...], axis=1, keepdims=True))
    inn[s4] = inn_tile
    marks = isel[...].astype(F32)
    beside = (
        jnp.sum(marks * inv[s4].T[:1], axis=1, keepdims=True),
        jnp.sum(marks * inn_tile[:1], axis=1, keepdims=True),
    )
    lane = lax.broadcasted_iota(jnp.int32, (rows, 128), 1)
    extra = jnp.zeros((rows, 128), F32)
    for n, value in enumerate(beside):
        for m in range(3):
            part = value.astype(BF).astype(F32)
            extra = jnp.where(lane == 3 * n + m, part, extra)
            value = value - part
    rall = r["rall"]
    rall[z, xl, c] = jnp.concatenate([dot_nn(isel[...], grads).astype(BF), extra.astype(BF)], axis=1)
    gather = Gather(lambda zz, xx, cc: rall.at[zz, xx, cc])

    gg[s4] = dot_nn(tsel[s4], grads).astype(BF)
    k_gg, k_inn = alloc(3), alloc(4)
    send(gg.at[s4], gg.at[s4], k_gg, twin)
    send(gg.at[s4], gg.at[s4], k_gg + 1, cross)
    for k in range(1, 4):
        send(inn.at[s4], inn.at[s4], k_inn + k, dev(z, *near(k), t))
    k_int, k_back, k_int2, k_back2 = alloc(nt), alloc(2 * nt), alloc(nt), alloc(nt)

    bs, br, bo = r["bs"], r["br"], r["bo"]
    depth_all = gg.shape[2]

    def back(half, xx):
        def one(tt):
            lines = gg[pl.ds(2 * xx, 2)].reshape(2 * texts, depth_all)
            return dot_nt(lines, wg[pl.ds(pl.multiple_of(tt * chunk, chunk), chunk), :])

        def step(n, carry):
            d = ny * (1 - n % 2) + (n + 1) // 2
            tt = to_t(d)
            bs[d, xx] = one(tt).astype(BF)
            rcopy(bs.at[d, xx], br.at[d, xx], k_back + 2 * d + half, dev(z, xl, c, tt)).start()
            return carry

        lax.fori_loop(0, nt - 1, step, 0)
        for d in range(1, nt):
            pending.append(rcopy(bs.at[d, xx], br.at[d, xx], k_back + 2 * d + half, dev(z, xl, c, to_t(d))))
        return one

    recv(gg.at[xl * 2 + 1 - c], k_gg)
    near_half = back(0, xl)
    gather.crossed()
    across, corner = gg.at[(1 - xl) * 2 + c], gg.at[(1 - xl) * 2 + 1 - c]
    recv(across, k_gg + 1)
    send(across, across, k_gg + 2, twin)
    for k in range(1, 4):
        xx, cc = near(k)
        recv(inn.at[xx * 2 + cc], k_inn + k)
    int_all[t] = inn[...]
    for d in range(1, nt):
        send(int_all.at[t], int_all.at[t], k_int + d, dev(z, xl, c, to_t(d)))
    recv(corner, k_gg + 2)
    far_half = back(1, 1 - xl)
    for i in range(1, n_right + 1):
        gather.step(i)
        if i == 1:
            bo[xl] = near_half(t)
            bo[1 - xl] = far_half(t)
            own_x = dot_nn(h_own, r["outer_v"][t])
            for d in range(1, nt):
                recv(own_r.at[d], k_own + d)
                own_x = own_x + own_r[d].astype(F32)
            own_x = own_x.astype(BF).astype(F32)
    gather.finish()

    routed = dot_nn(wanted[...], rall[...].reshape(total, rall.shape[4]))
    inv_row = routed[:, depth_all : depth_all + 1] + routed[:, depth_all + 1 : depth_all + 2]
    inv_row = inv_row + routed[:, depth_all + 2 : depth_all + 3]
    inn_row = routed[:, depth_all + 3 : depth_all + 4] + routed[:, depth_all + 4 : depth_all + 5]
    inn_row = inn_row + routed[:, depth_all + 5 : depth_all + 6]
    routed = routed[:, :depth_all].astype(BF)
    int_own = r["int_own"]
    int_own[t] = row_tile(inn_row)
    bs2, br2 = r["bs2"], r["br2"]
    for d in around:
        bs2[d] = dot_nt(routed, wg[pl.ds(pl.multiple_of(to_t(d) * chunk, chunk), chunk), :]).astype(BF)
        send(bs2.at[d], br2.at[d], k_back2 + d, dev(z, xl, c, to_t(d)))
        send(int_own.at[t], int_own.at[t], k_int2 + d, dev(z, xl, c, to_t(d)))
    own_back = dot_nt(routed, wg[pl.ds(pl.multiple_of(t * chunk, chunk), chunk), :])

    for d in range(1, nt):
        recv(int_all.at[from_t(d)], k_int + d)
    for d in range(1, nt):
        for half, xx in ((0, xl), (1, 1 - xl)):
            recv(br.at[d, xx], k_back + 2 * d + half)
        bo[...] += br[d].astype(F32)
    gt_s, gt_r = r["gt_s"], r["gt_r"]
    for o in range(4):
        tile = int_all[0, o]
        for d in range(1, nt):
            tile = tile + int_all[d, o]
        marks = tsel[o].astype(F32)
        inv_o = jnp.sum(marks * inv[o].T[:1], axis=1, keepdims=True)
        inn_o = jnp.sum(marks * tile[:1], axis=1, keepdims=True)
        x = dot_nn(tsel[o], xf[o * 128 : (o + 1) * 128, pl.ds(pl.multiple_of(t * chunk, chunk), chunk)])
        grad = inv_o * bo[o // 2, o % 2 * texts : (o % 2 + 1) * texts, :] - x * (inv_o * inv_o * inn_o / width)
        gt_s[o] = dot_tn(tsel[o], grad.astype(BF)).astype(BF).reshape(2, 64, chunk)
    k_gt, k_gr = alloc(4), alloc(4)
    for k in range(1, 4):
        xx, cc = near(k)
        send(gt_s.at[pl.ds(2 * xx, 2), cc], gt_r.at[s4], k_gt + k, dev(z, xx, cc, t))
    gt_r[s4] = gt_s[pl.ds(2 * xl, 2), c]

    for d in range(1, nt):
        recv(int_own.at[from_t(d)], k_int2 + d)
        recv(br2.at[d], k_back2 + d)
        own_back = own_back + br2[d].astype(F32)
    tile = int_own[0]
    for d in range(1, nt):
        tile = tile + int_own[d]
    grad = inv_row * own_back - own_x * (inv_row * inv_row * column_of(tile)[:, :1] / width)
    gr_s, gr_r = r["gr_s"], r["gr_r"]
    gr_s[...] = grad.astype(BF).reshape(4, rows, chunk)
    for k in range(1, 4):
        xx, cc = near(k)
        send(gr_s.at[xx * 2 + cc], gr_r.at[s4], k_gr + k, dev(z, xx, cc, t))
    gr_r[s4] = gr_s[s4]
    for k in range(1, 4):
        xx, cc = near(k)
        recv(gt_r.at[xx * 2 + cc], k_gt + k)
    for o in range(4):
        r["gtext"][:, :, o * chunk : (o + 1) * chunk] = gt_r[o]
    for k in range(1, 4):
        xx, cc = near(k)
        recv(gr_r.at[xx * 2 + cc], k_gr + k)
    for o in range(4):
        r["gimage"][:, o * chunk : (o + 1) * chunk] = gr_r[o]
    recv(att_r, k_att)
    r["attended"][c] = att_o[c]
    r["attended"][1 - c] = att_r[...]
    for copy in pending:
        copy.wait_send()


def per_device(
    patches,
    merge_gain,
    merge_bias,
    merge_inner,
    merge_outer,
    slot_target,
    text_embed,
    norm_gain,
    query_weight,
    key_weight,
    value_weight,
    attn_cotangent,
):
    nsec, nt = lax.axis_size("sec"), lax.axis_size("tp")
    nz, ny = nsec // 4, max(nt // 2, 1)
    rows, pw = patches.shape
    hid = merge_inner.shape[1]
    micro, tok, feat = text_embed.shape
    chunk = feat // 4
    seq = tok * nsec
    images = 4 * rows
    total = nz * images
    depth = query_weight.shape[0]
    heads = query_weight.shape[1] // HEAD_DIM
    cols = (heads + 2) * HEAD_DIM
    plane = 512

    vmem, anyspace = pl.BlockSpec(memory_space=pltpu.VMEM), pl.BlockSpec(memory_space=pl.ANY)
    n_right, n_left = nz // 2, max((nz - 1) // 2, 1)
    n_sem = 320
    ins = ["patches", "gain", "bias", "inner", "outer", "slot", "ngain", "text", "wq", "wk", "wv", "cot"]
    outs = ["attended", "gtext", "gimage"]
    scratch = dict(
        pall=((nt, rows, pw), BF),
        inner_v=(merge_inner.shape, BF),
        outer_v=((nt, hid, chunk), BF),
        a=((nt, 4, 2, tok, chunk), BF),
        wg=((nz * depth, cols), BF),
        d_out=((2, tok, heads * HEAD_DIM), BF),
        w_v=((depth, cols), BF),
        gain_v=((depth * nsec // 128, 128), F32),
        kcol=((total, 128), F32),
        wanted=((images, total), BF),
        tsel=((4, 128 - rows, 128), BF),
        isel=((rows, 128), BF),
        own_s=((nt, images, chunk), BF),
        own_r=((nt, images, chunk), BF),
        int_own=((nt, 8, 128), F32),
        bs2=((nt, images, chunk), BF),
        br2=((nt, images, chunk), BF),
        gr_s=((4, rows, chunk), BF),
        gr_r=((4, rows, chunk), BF),
        hall=((nz, 2, 2, rows, hid), BF),
        pick=((images, total), BF),
        place=((plane, images), BF),
        mask=((plane, chunk), F32),
        part_s=((nt, images, chunk), BF),
        part_r=((nt, images, chunk), BF),
        img=((nt, images, chunk), BF),
        xf=((plane, nt * chunk), BF),
        ss=((plane, 128), F32),
        ss_all=((4, 4, 8, 128), F32),
        inv=((4, 128, 128), F32),
        c_s=((3, 128, cols), BF),
        c_r=((3, 128, cols), BF),
        cn=((128, cols), F32),
        qs=((heads, 128, 128), BF),
        kv=((nz, 2, 128, 256), BF),
        dos=((heads, 128, 128), BF),
        ph=((heads, 128, seq), BF),
        ds=((heads, 128, seq), BF),
        att=((heads, 128, 128), BF),
        dq=((heads, 128, 128), BF),
        att_o=((2, tok, heads * HEAD_DIM), BF),
        att_r=((tok, heads * HEAD_DIM), BF),
        sr=((2, n_right, 128, 256), BF),
        rr=((2, n_right, 128, 256), BF),
        sl=((2, n_left, 128, 256), BF),
        rl=((2, n_left, 128, 256), BF),
        dkv=((nz, 2, 128, 256), F32),
        dx_s=((128, 256), BF),
        dx_r=((128, 256), BF),
        gg=((4, 128 - rows, cols), BF),
        inn=((4, 8, 128), F32),
        int_all=((nt, 4, 8, 128), F32),
        bs=((nt, 2, 2 * (128 - rows), chunk), BF),
        br=((nt, 2, 2 * (128 - rows), chunk), BF),
        bo=((2, 2 * (128 - rows), chunk), F32),
        gt_s=((4, 2, tok, chunk), BF),
        gt_r=((4, 2, tok, chunk), BF),
        rall=((nz, 2, 2, rows, cols + 128), BF),
    )
    names = ins + outs + list(scratch) + ["ssem", "rsem", "lsem", "n_sem"]
    call = pl.pallas_call(
        lambda *refs: kernel(nz, nt, ny, names, *refs, n_sem),
        out_shape=(
            jax.ShapeDtypeStruct((micro, tok, heads * HEAD_DIM), BF),
            jax.ShapeDtypeStruct((micro, tok, feat), BF),
            jax.ShapeDtypeStruct((rows, feat), BF),
        ),
        in_specs=[vmem if n in ("gain", "bias", "slot", "ngain") else anyspace for n in ins],
        out_specs=(vmem,) * 3,
        scratch_shapes=[pltpu.VMEM(shape, dtype) for shape, dtype in scratch.values()]
        + [
            pltpu.SemaphoreType.DMA((n_sem,)),
            pltpu.SemaphoreType.DMA((n_sem,)),
            pltpu.SemaphoreType.DMA((24,)),
        ],
        compiler_params=pltpu.CompilerParams(
            collective_id=0, has_side_effects=True, vmem_limit_bytes=56 * 1024 * 1024
        ),
        name="merged_step",
    )
    return call(
        patches,
        merge_gain,
        merge_bias,
        merge_inner,
        merge_outer,
        slot_target,
        norm_gain,
        text_embed,
        query_weight,
        key_weight,
        value_weight,
        attn_cotangent,
    )


def solution(mesh):
    return jax.shard_map(
        per_device,
        mesh=mesh,
        in_specs=(
            P("sec", "tp"),
            P(),
            P(),
            P(None, "tp"),
            P("tp", None),
            P(),
            P(None, "sec", "tp"),
            P(),
            P("sec", "tp"),
            P("sec", "tp"),
            P("sec", "tp"),
            P(None, "sec", "tp"),
        ),
        out_specs=(P(None, "sec", "tp"), P(None, "sec", "tp"), P("sec", "tp")),
        check_vma=False,
    )
```
